256 devices in a mesh: frames: 64 (over y_hi, z, x), heads: 4 (over y_lo, core).
Axes of the slice: x: 4, y: 4 (y_hi: 2, y_lo: 2; y = y_hi * 2 + y_lo), z: 8, core: 2. Of those that a mesh axis runs over, the one named last changes fastest.
Arguments:
- frame_q: bfloat16 [256, 256, 5120], P('frames', None, 'heads'), may hold values from -200 to 200
- frame_k: bfloat16 [256, 256, 5120], P('frames', None, 'heads'), may hold values from -8 to 8
- frame_v: bfloat16 [256, 256, 5120], P('frames', None, 'heads'), may hold values from -6 to 6
- keyframe_q: bfloat16 [2048, 5120], P(('frames', 'heads')), may hold values from -200 to 200
- keyframe_k: bfloat16 [2048, 5120], P(('frames', 'heads')), may hold values from -8 to 8
- keyframe_v: bfloat16 [2048, 5120], P(('frames', 'heads')), may hold values from -6 to 6
- neighbours: int32 [64, 2], P('frames'), may hold values from 0 to 7
Outputs:
- frame_out: bfloat16 [256, 256, 5120], P('frames', None, 'heads')
- keyframe_out: bfloat16 [2048, 5120], P('frames', 'heads')
The draws below stay inside these ranges and needn't reach their ends.
All inputs are finite; a program needn't handle non-finite values.
Results may differ from the reference program's by a relative error of at most 0.0047.
Values may be sent and summed in bfloat16 or wider, within the bound.
A program may use at most 128 MiB of HBM per device.

```python
import math
import jax
import jax.numpy as jnp
from jax import lax

HEAD_FEATURES = 128
D = 5120
FPD = 4
TPF = 256
FRAMES = 256
KF = 8
KTOK = 2048
GROUPS = 64


def frame_base(key):
    inner = jax.random.fold_in(key, 101)
    return jnp.clip(jax.random.normal(inner, (FRAMES, TPF, D), jnp.float32), -6.0, 6.0)


def anchor_base(key):
    inner = jax.random.fold_in(key, 202)
    return jnp.clip(jax.random.normal(inner, (KTOK, D), jnp.float32), -6.0, 6.0)


def draw_frame_k(key, part):
    base = frame_base(key)
    return base.astype(jnp.bfloat16)


def draw_frame_q(key, part):
    key = jax.random.fold_in(key, 4)
    values = jnp.clip(jax.random.normal(key, (FRAMES, TPF, D), jnp.float32), -6.0, 6.0)
    return values.astype(jnp.bfloat16)


def draw_keyframe_k(key, part):
    base = anchor_base(key)
    return base.astype(jnp.bfloat16)


def draw_keyframe_q(key, part):
    key = jax.random.fold_in(key, 6)
    values = jnp.clip(jax.random.normal(key, (KTOK, D), jnp.float32), -6.0, 6.0)
    return values.astype(jnp.bfloat16)


def with_ends(entries, key, low, high):
    place = [jax.random.randint(jax.random.fold_in(key, axis), (), 0, length) for axis, length in enumerate(entries.shape)]
    longest = entries.shape.index(max(entries.shape))
    beside = place[:longest] + [(place[longest] + 1) % entries.shape[longest]] + place[longest + 1:]
    return entries.at[tuple(place)].set(low).at[tuple(beside)].set(high)


def level_of(rng, extent, pieces, least, largest):
    def one(axis_at, blocks):
        draws = jax.random.uniform(jax.random.fold_in(jax.random.fold_in(rng, 6), axis_at), (blocks,), jnp.float32, least / len(pieces), largest / len(pieces))
        return jnp.repeat(jnp.exp(draws), extent[axis_at] // blocks).reshape((-1,) + (1,) * (len(extent) - axis_at - 1))

    gain = one(*pieces[0])
    for cut in pieces[1:]:
        gain = gain * one(*cut)
    return gain


def bell_draw(stream_key, extent, scale, bound, pieces=(), held_as=jnp.bfloat16):
    array = scale * jax.random.normal(stream_key, extent, jnp.float32)
    if pieces:
        array = array * level_of(stream_key, extent, pieces, -0.22, 0.18)
    return jnp.clip(array, -bound, bound).astype(held_as)


def setup_inputs(seed: int = 0) -> dict:
    streams_of = jax.random.split(jax.random.key(seed), 8)
    return {
        "frame_q": draw_frame_q(jax.random.fold_in(streams_of[7], 71), 0),
        "frame_k": draw_frame_k(jax.random.fold_in(streams_of[7], 71), 0),
        "frame_v": bell_draw(streams_of[2], (FRAMES, TPF, D), 1.0, 6.0, ((0, 64), (2, 4))),
        "keyframe_q": draw_keyframe_q(jax.random.fold_in(streams_of[7], 71), 0),
        "keyframe_k": draw_keyframe_k(jax.random.fold_in(streams_of[7], 71), 0),
        "keyframe_v": bell_draw(streams_of[5], (KTOK, D), 1.0, 6.0, ((0, 256),)),
        "neighbours": with_ends(jax.random.randint(streams_of[6], (GROUPS, 2), 0, KF), jax.random.fold_in(streams_of[6], 1), 0, KF - 1).astype(jnp.int32),
    }


def attend(queries, keys_set, values_set, usable):
    row_count = queries.shape[0]
    key_count = keys_set.shape[0]
    head_count = queries.shape[1] // HEAD_FEATURES
    query_head_rows = queries.reshape(row_count, head_count, HEAD_FEATURES).astype(jnp.float32)
    key_head_rows = keys_set.reshape(key_count, head_count, HEAD_FEATURES).astype(jnp.float32)
    value_head_rows = values_set.reshape(key_count, head_count, HEAD_FEATURES).astype(jnp.float32)
    score_matrix = jnp.einsum('gia,xia->igx', query_head_rows, key_head_rows) / math.sqrt(HEAD_FEATURES)
    score_matrix = jnp.where(usable[None, None, :], score_matrix, -jnp.inf)
    highest = lax.optimization_barrier(jnp.max(score_matrix, axis=-1, keepdims=True))
    weights = jnp.exp(score_matrix - highest)
    totals = lax.optimization_barrier(jnp.sum(weights, axis=-1))
    rounded_scores = lax.optimization_barrier(weights.astype(jnp.bfloat16)).astype(jnp.float32)
    blended_output = jnp.einsum('wqt,twx->qwx', rounded_scores, value_head_rows)
    result = blended_output / jnp.transpose(totals)[:, :, None]
    return result.reshape(row_count, head_count * HEAD_FEATURES).astype(jnp.bfloat16)

def reference(frame_q, frame_k, frame_v, keyframe_q, keyframe_k, keyframe_v, neighbours):
    anchor_k = keyframe_k.reshape(KF, TPF, D)
    anchor_v = keyframe_v.reshape(KF, TPF, D)
    padded_k = jnp.pad(frame_k, ((1, 1), (0, 0), (0, 0)))
    padded_v = jnp.pad(frame_v, ((1, 1), (0, 0), (0, 0)))

    def one_frame(frame_index):
        group = frame_index // FPD
        left_id = neighbours[group, 0]
        right_id = neighbours[group, 1]
        window_k = lax.dynamic_slice_in_dim(padded_k, frame_index, 3, 0).reshape(3 * TPF, D)
        window_v = lax.dynamic_slice_in_dim(padded_v, frame_index, 3, 0).reshape(3 * TPF, D)
        keys_set = jnp.concatenate([window_k, anchor_k[left_id], anchor_k[right_id]], axis=0)
        values_set = jnp.concatenate([window_v, anchor_v[left_id], anchor_v[right_id]], axis=0)
        usable = jnp.concatenate([jnp.full((TPF,), frame_index > 0), jnp.ones((TPF,), jnp.bool_), jnp.full((TPF,), frame_index < FRAMES - 1), jnp.ones((2 * TPF,), jnp.bool_)])
        return attend(frame_q[frame_index], keys_set, values_set, usable)
    frame_out = lax.map(one_frame, jnp.arange(FRAMES, dtype=jnp.int32))
    keyframe_out = attend(keyframe_q, keyframe_k, keyframe_v, jnp.ones((KTOK,), jnp.bool_))
    return (frame_out, keyframe_out)
```

```python
import math

import jax
import jax.numpy as jnp
from jax import lax
from jax.experimental import pallas as pl
from jax.experimental.pallas import tpu as pltpu
from jax.sharding import PartitionSpec as P

HEAD = 128
XN, ZN, YN = 4, 8, 2
HN = 4
HEADS = 10
CHUNKS = 5
WIDE = 256
PER = WIDE // HEAD
TOK = 256
FEAT = HEADS * HEAD
SCALE = math.log2(math.e) / math.sqrt(HEAD)
F32 = jnp.float32
BF16 = jnp.bfloat16
NT = (((1,), (1,)), ((), ()))
SPANS = ((0, 2), (0, 3), (1, 3), (2, 2))
MESH = pl.DeviceIdType.MESH


def kernel(
    q_hbm, k_hbm, v_hbm, kv_hbm, kq_hbm, nb_hbm,
    out_hbm, kout,
    q, k, v, edge, arr, arrq, ring, send, got, o_st, m_st, l_st, sc, sc_m, out_v,
    qx, ox_s, ox_r, st_s, st_r, nb, nb_s,
    load_sem, out_sem, edge_ss, edge_rs, a_ss, a_rs, aq_ss, aq_rs, nb_ss, nb_rs, loc_sem,
    r_ss, r_rs, s_ss, s_rs, qx_ss, qx_rs, ox_ss, ox_rs, st_ss, st_rs,
):
    f = lax.axis_index("frames")
    hd = lax.axis_index("heads")
    x = f % XN
    z = (f // XN) % ZN
    yh = f // (XN * ZN)
    groups = XN * ZN * YN

    def dev(yh_, z_, x_, h_):
        return ((yh_ * ZN + z_) * XN + x_, h_)

    def remote(src, dst, ss, rs, to):
        return pltpu.make_async_remote_copy(
            src_ref=src, dst_ref=dst, send_sem=ss, recv_sem=rs, device_id=to, device_id_type=MESH
        )

    def loads(ch):
        c = pl.ds(pl.multiple_of(ch * WIDE, WIDE), WIDE)
        return [
            pltpu.make_async_copy(a.at[:, :, c], b.at[:, :, c], load_sem.at[ch, n])
            for n, (a, b) in enumerate(((q_hbm, q), (k_hbm, k), (v_hbm, v)))
        ]

    for ch in range(CHUNKS):
        for cp in loads(ch):
            cp.start()

    nxt = ((f + 1) % groups, hd)
    prv = ((f + groups - 1) % groups, hd)
    mine8 = yh * HN + hd

    def part8(d):
        o = (mine8 + d) % (YN * HN)
        return o // HN, o % HN, o

    zr = dev(yh, (z + 1) % ZN, x, hd)
    zl = dev(yh, (z + ZN - 1) % ZN, x, hd)

    def xpart(j):
        return dev(yh, z, (x + j) % XN, hd)

    barrier = pltpu.get_barrier_semaphore()
    partners = [nxt, prv, zr, zl] + [xpart(j) for j in (1, 2, 3)]
    for d in range(1, 8):
        y8, h8, _ = part8(d)
        partners.append(dev(y8, z, x, h8))
    for p_ in partners:
        pl.semaphore_signal(barrier, inc=1, device_id=p_, device_id_type=MESH)
    pl.semaphore_wait(barrier, len(partners))

    def cols(h_):
        return pl.ds(pl.multiple_of(h_ * FEAT, FEAT), FEAT)

    a_copies, aq_copies = [], []
    for d in range(1, 8):
        y8, h8, o = part8(d)
        a_copies.append(remote(kv_hbm.at[:, cols(h8)], arr.at[mine8], a_ss.at[d], a_rs.at[mine8], dev(y8, z, x, h8)))
    for d in range(1, HN):
        h4 = (hd + d) % HN
        aq_copies.append(remote(kq_hbm.at[:, cols(h4)], arrq.at[hd], aq_ss.at[d], aq_rs.at[hd], dev(yh, z, x, h4)))
    nb_copies = [remote(nb_hbm, nb.at[x], nb_ss.at[j], nb_rs.at[x], xpart(j)) for j in (1, 2, 3)]
    a_own = pltpu.make_async_copy(kv_hbm.at[:, cols(hd)], arr.at[mine8], loc_sem.at[0])
    aq_own = pltpu.make_async_copy(kq_hbm.at[:, cols(hd)], arrq.at[hd], loc_sem.at[1])
    nb_own = pltpu.make_async_copy(nb_hbm, nb.at[x], loc_sem.at[2])
    for cp in a_copies + aq_copies + nb_copies + [a_own, aq_own, nb_own]:
        cp.start()

    edge_copies = [
        remote(k_hbm.at[3], edge.at[0, 0], edge_ss.at[0, 0], edge_rs.at[0, 0], nxt),
        remote(k_hbm.at[0], edge.at[1, 0], edge_ss.at[1, 0], edge_rs.at[1, 0], prv),
        remote(v_hbm.at[3], edge.at[0, 1], edge_ss.at[0, 1], edge_rs.at[0, 1], nxt),
        remote(v_hbm.at[0], edge.at[1, 1], edge_ss.at[1, 1], edge_rs.at[1, 1], prv),
    ]
    for cp in edge_copies:
        cp.start()

    def ring_copies(s):
        a = (z + ZN - s) % ZN
        b = (z + s) % ZN
        src_r = ring.at[a] if s < 3 else ring.at[a, 0]
        src_l = ring.at[b] if s < 3 else ring.at[b, 1]
        return (
            remote(src_r, src_r, r_ss.at[0, s], r_rs.at[0, s], zr),
            remote(src_l, src_l, r_ss.at[1, s], r_rs.at[1, s], zl),
        )

    qx_copies = [remote(qx.at[x], qx.at[x], qx_ss.at[j], qx_rs.at[x], xpart(j)) for j in (1, 2, 3)]

    def service_a():
        a_own.wait()
        aq_own.wait()
        nb_own.wait()
        for d in range(1, 8):
            _, _, o = part8(d)
            remote(arr.at[o], arr.at[o], a_ss.at[d], a_rs.at[o], zr).wait_recv()
        for d in range(1, HN):
            h4 = (hd + d) % HN
            remote(arrq.at[h4], arrq.at[h4], aq_ss.at[d], aq_rs.at[h4], zr).wait_recv()
        for y_ in range(YN):
            for j in range(HN // 2):
                t0 = arr[y_ * HN + 2 * j].astype(F32)
                t1 = arr[y_ * HN + 2 * j + 1].astype(F32)
                r = pl.ds(16 * j, 16)
                ring[z, 0, y_, r] = jnp.concatenate([t0[:8], t1[:8]], 0).astype(BF16)
                ring[z, 1, y_, r] = jnp.concatenate([t0[8:], t1[8:]], 0).astype(BF16)
        for cp in ring_copies(0):
            cp.start()
        for j in range(HN // 2):
            qx[x, pl.ds(16 * j, 16)] = jnp.concatenate([arrq[2 * j], arrq[2 * j + 1]], 0).astype(BF16)
        for cp in qx_copies:
            cp.start()

    def service_ring(s):
        for cp in ring_copies(s - 1):
            cp.wait_recv()
        for cp in ring_copies(s):
            cp.start()

    def cs(h):
        return pl.ds(pl.multiple_of(h * HEAD, HEAD), HEAD)

    def run(units):
        units[0][0](0)
        for j in range(len(units)):
            if j + 1 < len(units):
                units[j + 1][0]((j + 1) % 2)
            units[j][1](j % 2)

    def unit(get_q, get_k, get_v, rows, n, fold, finish, valid=None):
        def scores(slot):
            s = lax.dot_general(get_q(), get_k(), NT, preferred_element_type=F32)
            if valid is not None:
                s = jnp.where(valid, s, -jnp.inf)
            sc[slot, 0:rows, 0:n] = s
            m = jnp.max(s, axis=1, keepdims=True)
            if fold is not None:
                m = jnp.maximum(m, fold[0]())
            sc_m[slot, 0:rows] = m

        def values(slot):
            m = sc_m[slot, 0:rows]
            p = jnp.exp2((sc[slot, 0:rows, 0:n] - m) * SCALE)
            l = jnp.sum(p, axis=1, keepdims=True)
            o = jnp.dot(p.astype(BF16), get_v(), preferred_element_type=F32)
            if fold is not None:
                a = jnp.exp2((fold[0]() - m) * SCALE)
                l = l + fold[1]() * a
                o = o + fold[2]() * a
            finish(m, l, o)

        return scores, values

    def state(h, i):
        return (lambda: m_st[h, i], lambda: l_st[h, i], lambda: o_st[h, i])

    def keep(h, i):
        def finish(m, l, o):
            m_st[h, i] = m
            l_st[h, i] = l
            o_st[h, i] = o

        return finish

    def local_unit(h, i):
        a, n = SPANS[i]
        c = cs(h)
        return unit(
            lambda: q[i, :, c],
            lambda: k[a : a + n, :, c].reshape(n * TOK, HEAD),
            lambda: v[a : a + n, :, c].reshape(n * TOK, HEAD),
            TOK, n * TOK, None, keep(h, i),
        )

    def local_chunk(ch, _):
        for cp in loads(ch):
            cp.wait()
        run([local_unit(ch * PER + j, i) for j in range(PER) for i in range(4)])

        @pl.when(ch == 1)
        def _():
            service_a()

        @pl.when(ch == 3)
        def _():
            service_ring(1)

        return 0

    lax.fori_loop(0, CHUNKS, local_chunk, 0)
    service_ring(2)
    service_ring(3)
    for j in (1, 2, 3):
        xx = (x + j) % XN
        remote(nb.at[xx], nb.at[xx], nb_ss.at[j], nb_rs.at[xx], zr).wait_recv()
        remote(qx.at[xx], qx.at[xx], qx_ss.at[j], qx_rs.at[xx], zr).wait_recv()
    nb_smem = pltpu.make_async_copy(nb, nb_s, loc_sem.at[3])
    nb_smem.start()
    nb_smem.wait()
    for cp in ring_copies(3):
        cp.wait_recv()

    def pick(dst, xx):
        for side in range(2):
            kf = nb_s[xx, side, 0]
            for half in range(2):
                for kind in range(2):
                    blk = ring[2 * (kf % 4) + half, kind, kf // 4]
                    for ch in range(CHUNKS):
                        dst(ch)[side, kind, pl.ds(32 * half, 32)] = blk[:, ch * WIDE : (ch + 1) * WIDE]

    def send_copy(ch, j):
        return remote(send.at[j - 1, ch], got.at[ch, x], s_ss.at[ch, j], s_rs.at[ch, x], xpart(j))

    for j in (1, 3, 2):
        pick(lambda ch: send.at[j - 1, ch], (x + j) % XN)
    for ch in range(CHUNKS):
        for j in (1, 3, 2):
            send_copy(ch, j).start()
    pick(lambda ch: got.at[ch, x], x)

    st_s[...] = jnp.zeros_like(st_s)

    def joint_unit(h):
        c = cs(h)

        def finish(m, l, o):
            ox_s[:, :, c] = (o / l).astype(BF16).reshape(XN, 32, HEAD)
            lane = lax.broadcasted_iota(jnp.int32, (XN * 32, HEAD), 1) == h
            st_s[:, 0] = jnp.where(lane, m, st_s[:, 0].reshape(XN * 32, HEAD)).reshape(XN, 32, HEAD)
            st_s[:, 1] = jnp.where(lane, l, st_s[:, 1].reshape(XN * 32, HEAD)).reshape(XN, 32, HEAD)

        return unit(
            lambda: qx[:, :, c].reshape(XN * 32, HEAD),
            lambda: ring[:, 0, :, :, c].reshape(512, HEAD),
            lambda: ring[:, 1, :, :, c].reshape(512, HEAD),
            XN * 32, 512, None, finish,
        )

    def joint_chunk(ch, _):
        run([joint_unit(ch * PER + j) for j in range(PER)])
        return 0

    lax.fori_loop(0, CHUNKS, joint_chunk, 0)
    ox_copies, st_copies = [], []
    for j in (1, 2, 3):
        xx = (x + j) % XN
        ox_copies.append(remote(ox_s.at[xx], ox_r.at[x], ox_ss.at[j], ox_rs.at[x], xpart(j)))
        st_copies.append(remote(st_s.at[xx], st_r.at[x], st_ss.at[j], st_rs.at[x], xpart(j)))
    for cp in ox_copies + st_copies:
        cp.start()
    ox_r[x] = ox_s[x]
    st_r[x] = st_s[x]

    for cp in edge_copies:
        cp.wait_recv()

    def edge_unit(h, e):
        i = 3 * e
        c = cs(h)
        return unit(
            lambda: q[i, :, c], lambda: edge[e, 0, :, c], lambda: edge[e, 1, :, c],
            TOK, TOK, state(h, i), keep(h, i),
            valid=(f > 0) if e == 0 else (f < groups - 1),
        )

    def edge_chunk(ch, _):
        run([edge_unit(ch * PER + j, e) for j in range(PER) for e in range(2)])
        return 0

    lax.fori_loop(0, CHUNKS, edge_chunk, 0)

    def out_copy(ch):
        c = pl.ds(pl.multiple_of(ch * WIDE, WIDE), WIDE)
        return pltpu.make_async_copy(out_v.at[:, :, c], out_hbm.at[:, :, c], out_sem.at[ch])

    def last_unit(ch, j, i):
        h = ch * PER + j
        c = cs(h)
        w = slice(j * HEAD, (j + 1) * HEAD)

        def finish(m, l, o):
            out_v[i, :, c] = (o / l).astype(BF16)

        return unit(
            lambda: q[i, :, c],
            lambda: got[ch, :, :, 0, :, w].reshape(512, HEAD),
            lambda: got[ch, :, :, 1, :, w].reshape(512, HEAD),
            TOK, 512, state(h, i), finish,
        )

    def last_chunk(ch, _):
        for j in (1, 2, 3):
            xx = (x + j) % XN
            remote(got.at[ch, xx], got.at[ch, xx], s_ss.at[ch, j], s_rs.at[ch, xx], zr).wait_recv()
        run([last_unit(ch, j, i) for j in range(PER) for i in range(4)])
        out_copy(ch).start()
        return 0

    lax.fori_loop(0, CHUNKS, last_chunk, 0)

    for j in (1, 2, 3):
        xx = (x + j) % XN
        remote(ox_r.at[xx], ox_r.at[xx], ox_ss.at[j], ox_rs.at[xx], zr).wait_recv()
        remote(st_r.at[xx], st_r.at[xx], st_ss.at[j], st_rs.at[xx], zr).wait_recv()
    m_all = st_r[:, 0]
    w_all = jnp.exp2((m_all - jnp.max(m_all, axis=0, keepdims=True)) * SCALE) * st_r[:, 1]
    total = jnp.sum(w_all, axis=0, keepdims=True)
    w_all = w_all / jnp.where(total > 0, total, 1.0)
    for h in range(HEADS):
        acc = jnp.zeros((32, HEAD), F32)
        for cl in range(XN):
            acc = acc + ox_r[cl, :, h * HEAD : (h + 1) * HEAD].astype(F32) * w_all[cl, :, h : h + 1]
        kout[:, h * HEAD : (h + 1) * HEAD] = acc.astype(BF16)

    for cp in a_copies + aq_copies + nb_copies + edge_copies + qx_copies + ox_copies + st_copies:
        cp.wait_send()
    for s in range(4):
        for cp in ring_copies(s):
            cp.wait_send()
    for ch in range(CHUNKS):
        for j in (1, 2, 3):
            send_copy(ch, j).wait_send()
        out_copy(ch).wait()


def local(frame_q, frame_k, frame_v, keyframe_q, keyframe_k, keyframe_v, neighbours):
    kv = jnp.concatenate([keyframe_k, keyframe_v], axis=0)
    kq = keyframe_q.astype(F32)
    ids = jnp.pad(jnp.broadcast_to(neighbours.reshape(2, 1), (2, 128)), ((0, 6), (0, 0)))
    dma = pltpu.SemaphoreType.DMA
    any_ = pl.BlockSpec(memory_space=pl.ANY)
    vm = pltpu.VMEM
    frame_out, keyframe_out = pl.pallas_call(
        kernel,
        out_shape=(
            jax.ShapeDtypeStruct(frame_q.shape, BF16),
            jax.ShapeDtypeStruct((32, FEAT), BF16),
        ),
        in_specs=[any_] * 6,
        out_specs=(any_, pl.BlockSpec(memory_space=pltpu.VMEM)),
        scratch_shapes=[
            vm((4, TOK, FEAT), BF16), vm((4, TOK, FEAT), BF16), vm((4, TOK, FEAT), BF16),
            vm((2, 2, TOK, FEAT), BF16),
            vm((YN * HN, 16, FEAT), BF16),
            vm((HN, 8, FEAT), F32),
            vm((ZN, 2, YN, 32, FEAT), BF16),
            vm((3, CHUNKS, 2, 2, 64, WIDE), BF16),
            vm((CHUNKS, XN, 2, 2, 64, WIDE), BF16),
            vm((HEADS, 4, TOK, HEAD), F32),
            vm((HEADS, 4, TOK, 1), F32), vm((HEADS, 4, TOK, 1), F32),
            vm((2, TOK, 3 * TOK), F32), vm((2, TOK, 1), F32),
            vm((4, TOK, FEAT), BF16),
            vm((XN, 32, FEAT), BF16),
            vm((XN, 32, FEAT), BF16), vm((XN, 32, FEAT), BF16),
            vm((XN, 2, 32, HEAD), F32), vm((XN, 2, 32, HEAD), F32),
            vm((XN, 8, 128), jnp.int32), pltpu.SMEM((XN, 8, 128), jnp.int32),
            dma((CHUNKS, 3)), dma((CHUNKS,)), dma((2, 2)), dma((2, 2)),
            dma((8,)), dma((8,)), dma((4,)), dma((4,)), dma((4,)), dma((4,)), dma((4,)),
            dma((2, 4)), dma((2, 4)), dma((CHUNKS, 4)), dma((CHUNKS, 4)),
            dma((4,)), dma((4,)), dma((4,)), dma((4,)), dma((4,)), dma((4,)),
        ],
        compiler_params=pltpu.CompilerParams(
            collective_id=0, has_side_effects=True, vmem_limit_bytes=60 * 2**20
        ),
    )(frame_q, frame_k, frame_v, kv, kq, ids)
    return frame_out, keyframe_out


def solution(mesh):
    placed = (
        P("frames", None, "heads"),
        P("frames", None, "heads"),
        P("frames", None, "heads"),
        P(("frames", "heads"), None),
        P(("frames", "heads"), None),
        P(("frames", "heads"), None),
        P("frames", None),
    )
    return jax.shard_map(
        local,
        mesh=mesh,
        in_specs=placed,
        out_specs=(P("frames", None, "heads"), P("frames", "heads")),
        check_vma=False,
    )
```

```python
import math

import jax
import jax.numpy as jnp
from jax import lax
from jax.experimental import pallas as pl
from jax.experimental.pallas import tpu as pltpu
from jax.sharding import PartitionSpec as P

HEAD = 128
XN, ZN, YN = 4, 8, 2
HN = 4
HEADS = 10
CHUNKS = 5
WIDE = 256
PER = WIDE // HEAD
TOK = 256
FEAT = HEADS * HEAD
SCALE = math.log2(math.e) / math.sqrt(HEAD)
F32 = jnp.float32
BF16 = jnp.bfloat16
NT = (((1,), (1,)), ((), ()))
SPANS = ((0, 2), (0, 3), (1, 3), (2, 2))
MESH = pl.DeviceIdType.MESH


def kernel(
    q_hbm, k_hbm, v_hbm, kf_q, kf_k, kf_v, ids,
    out_hbm, kout,
    q, k, v, edge, kv, kq, arr, arrq, ringk, ringv, sndk, sndv, gotk, gotv,
    o_st, m_st, l_st, sc, sc_m, out_v, qx, ox_s, ox_r, st_s, st_r, nb_v, nb, nb_s,
    load_sem, out_sem, edge_ss, edge_rs, fwd_ss, fwd_rs, a_ss, a_rs, aq_ss, aq_rs, nb_ss, nb_rs, loc_sem,
    r_ss, r_rs, sk_ss, sk_rs, sv_ss, sv_rs, qx_ss, qx_rs, ox_ss, ox_rs, st_ss, st_rs,
):
    f = lax.axis_index("frames")
    hd = lax.axis_index("heads")
    x = f % XN
    z = (f // XN) % ZN
    y = f // (XN * ZN)
    xp = x % 2
    groups = XN * ZN * YN

    def dev(y_, z_, x_, h_):
        return ((y_ * ZN + z_) * XN + x_, h_)

    def remote(src, dst, ss, rs, to):
        return pltpu.make_async_remote_copy(
            src_ref=src, dst_ref=dst, send_sem=ss, recv_sem=rs, device_id=to, device_id_type=MESH
        )

    def loads(ch):
        c = pl.ds(pl.multiple_of(ch * WIDE, WIDE), WIDE)
        return [
            pltpu.make_async_copy(a.at[:, :, c], b.at[:, :, c], load_sem.at[ch, n])
            for n, (a, b) in enumerate(((q_hbm, q), (k_hbm, k), (v_hbm, v)))
        ]

    for ch in range(CHUNKS):
        for cp in loads(ch):
            cp.start()

    zr = dev(y, (z + 1) % ZN, x, hd)
    zl = dev(y, (z + ZN - 1) % ZN, x, hd)
    fwd_to = (((f + XN) % groups, hd), ((f + groups - XN) % groups, hd))
    yo = (y + 1) % YN
    right, left = (x + 1) % XN, (x + XN - 1) % XN
    sel = [dev(yo, z, x, hd), dev(y, z, right, hd), dev(y, z, left, hd), dev(yo, z, right, hd), dev(yo, z, left, hd)]
    back = (0, 2, 1, 4, 3)
    barrier = pltpu.get_barrier_semaphore()
    near = []
    me16 = y * HN + hd
    for d in range(1, 16):
        o = (me16 + d) % 8
        near.append(dev(o // HN, z, (x + 2 * (d // 8)) % XN, o % HN))
    partners = near + sel[1:] + [zr, zl] + list(fwd_to)
    for p_ in partners:
        pl.semaphore_signal(barrier, inc=1, device_id=p_, device_id_type=MESH)

    kv[...] = jnp.concatenate([kf_k[...].astype(F32), kf_v[...].astype(F32)], 0).astype(BF16)
    kq[...] = kf_q[...].astype(F32)
    row = lax.broadcasted_iota(jnp.int32, (8, 128), 0)
    nb_v[...] = jnp.where(row == 0, ids[0, 0], ids[0, 1])
    pl.semaphore_wait(barrier, len(partners))

    def cols(h_):
        return pl.ds(pl.multiple_of(h_ * FEAT, FEAT), FEAT)

    ys, hp = hd // 2, hd % 2

    def a_copy(i, xs, h_):
        slot = y * 4 + xs * 2 + hp
        return remote(
            kv.at[:, cols(h_)], arr.at[slot], a_ss.at[i], a_rs.at[slot], dev(ys, z, (x + 2 * xs) % XN, h_)
        )

    a_copies = [a_copy(d, 0, (hd + d) % HN) for d in range(1, HN)] + [a_copy(4 + d, 1, d) for d in range(HN)]
    a_self = a_copy(0, 0, hd)
    own_slot = y * 4 + hp
    a_here = pltpu.make_async_copy(kv.at[:, cols(hd)], arr.at[own_slot], a_rs.at[own_slot])
    stays = ys == y

    for cp in a_copies:
        cp.start()

    @pl.when(stays)
    def _():
        a_here.start()

    @pl.when(jnp.logical_not(stays))
    def _():
        a_self.start()

    aq_copies = [
        remote(kq.at[:, cols((hd + d) % HN)], arrq.at[hd], aq_ss.at[d], aq_rs.at[hd], dev(y, z, x, (hd + d) % HN))
        for d in range(1, HN)
    ]
    nb_copies = [remote(nb_v, nb.at[back[i]], nb_ss.at[i], nb_rs.at[back[i]], sel[i]) for i in range(5)]
    aq_own = pltpu.make_async_copy(kq.at[:, cols(hd)], arrq.at[hd], loc_sem.at[0])
    nb_own = pltpu.make_async_copy(nb_v, nb.at[5], loc_sem.at[1])
    for cp in aq_copies + nb_copies + [aq_own, nb_own]:
        cp.start()

    edge_copies = [
        remote(k_hbm.at[3], edge.at[0, 0], edge_ss.at[0, 0], edge_rs.at[0, 0], sel[1]),
        remote(k_hbm.at[0], edge.at[1, 0], edge_ss.at[1, 0], edge_rs.at[1, 0], sel[2]),
        remote(v_hbm.at[3], edge.at[0, 1], edge_ss.at[0, 1], edge_rs.at[0, 1], sel[1]),
        remote(v_hbm.at[0], edge.at[1, 1], edge_ss.at[1, 1], edge_rs.at[1, 1], sel[2]),
    ]
    for cp in edge_copies:
        cp.start()

    def fwd_copy(e, ch, kind):
        c = pl.ds(pl.multiple_of(ch * WIDE, WIDE), WIDE)
        return remote(
            edge.at[e, kind, :, c], edge.at[2 + e, kind, :, c], fwd_ss.at[ch, kind], fwd_rs.at[ch, kind], fwd_to[e]
        )

    def each_end(fn):
        for e, end in ((0, 0), (1, XN - 1)):
            @pl.when(x == end)
            def _():
                fn(e)

    rings = (ringk, ringv)

    def ring_copies(part, s):
        kind, ysrc = part // 2, part % 2
        r = rings[kind]
        a = (z + ZN - s) % ZN
        b = (z + s) % ZN
        src_r = r.at[a, ysrc] if s < 3 else r.at[a, ysrc, 0:16]
        src_l = r.at[b, ysrc] if s < 3 else r.at[b, ysrc, 16:32]
        return (
            remote(src_r, src_r, r_ss.at[0, part, s], r_rs.at[0, part, s], zr),
            remote(src_l, src_l, r_ss.at[1, part, s], r_rs.at[1, part, s], zl),
        )

    quad = [(a, b) for a, b in ((0, 1), (1, 0), (1, 1))]
    gid = xp * 2 + y

    def quad_dev(a, b):
        return dev((y + b) % 2, z, x - xp + (xp + a) % 2, hd)

    def quad_gid(a, b):
        return ((xp + a) % 2) * 2 + (y + b) % 2

    qx_copies = [
        remote(qx.at[gid], qx.at[gid], qx_ss.at[n], qx_rs.at[gid], quad_dev(a, b)) for n, (a, b) in enumerate(quad)
    ]

    def service_a():
        for slot in range(8):
            remote(arr.at[slot], arr.at[slot], a_ss.at[slot], a_rs.at[slot], zr).wait_recv()
        for ysrc in range(YN):
            for j in range(2):
                t0 = arr[ysrc * 4 + 2 * j].astype(F32)
                t1 = arr[ysrc * 4 + 2 * j + 1].astype(F32)
                r = pl.ds(16 * j, 16)
                ringk[z, ysrc, r] = jnp.concatenate([t0[:8], t1[:8]], 0).astype(BF16)
                ringv[z, ysrc, r] = jnp.concatenate([t0[8:], t1[8:]], 0).astype(BF16)
        for part in (0, 1):
            for cp in ring_copies(part, 0):
                cp.start()

    def service_q():
        aq_own.wait()
        nb_own.wait()
        for d in range(1, HN):
            h4 = (hd + d) % HN
            remote(arrq.at[h4], arrq.at[h4], aq_ss.at[d], aq_rs.at[h4], zr).wait_recv()
        for j in range(HN // 2):
            qx[gid, pl.ds(16 * j, 16)] = jnp.concatenate([arrq[2 * j], arrq[2 * j + 1]], 0).astype(BF16)
        for cp in qx_copies:
            cp.start()

    def service_ring(part, s):
        for cp in ring_copies(part, s - 1):
            cp.wait_recv()
        for cp in ring_copies(part, s):
            cp.start()

    def cs(h):
        return pl.ds(pl.multiple_of(h * HEAD, HEAD), HEAD)

    def run(units):
        units[0][0](0)
        for j in range(len(units)):
            if j + 1 < len(units):
                units[j + 1][0]((j + 1) % 2)
            units[j][1](j % 2)

    def unit(get_q, parts, rows, fold, finish):
        def scores(slot):
            qq = get_q()
            at, top = 0, None
            for get_k, _, n, valid in parts:
                s = lax.dot_general(qq, get_k(), NT, preferred_element_type=F32)
                if valid is not None:
                    s = jnp.where(valid, s, -jnp.inf)
                sc[slot, 0:rows, at : at + n] = s
                for t in range(0, n, HEAD):
                    piece = s[:, t : t + HEAD]
                    top = piece if top is None else jnp.maximum(top, piece)
                at += n
            m = jnp.broadcast_to(jnp.max(top, axis=1, keepdims=True), (rows, HEAD))
            if fold is not None:
                m = jnp.maximum(m, fold[0]())
            sc_m[slot, 0:rows] = m

        def values(slot):
            m = sc_m[slot, 0:rows]
            at, l, o = 0, None, None
            for _, get_v, n, _ in parts:
                ps = []
                for t in range(at, at + n, HEAD):
                    p = jnp.exp2((sc[slot, 0:rows, t : t + HEAD] - m) * SCALE)
                    l = p if l is None else l + p
                    ps.append(p.astype(BF16))
                d = jnp.dot(jnp.concatenate(ps, axis=1), get_v(), preferred_element_type=F32)
                o = d if o is None else o + d
                at += n
            if fold is not None:
                a = jnp.exp2((fold[0]() - m) * SCALE)
                l = l + fold[1]() * a
                o = o + fold[2]() * a
            finish(m, l, o)

        return scores, values

    def local_unit(h, i):
        a, n = SPANS[i]
        c = cs(h)

        def finish(m, l, o):
            m_st[h, i] = m
            l_st[h, i] = l
            o_st[h, i] = o

        return unit(
            lambda: q[i, :, c],
            [(
                lambda: k[a : a + n, :, c].reshape(n * TOK, HEAD),
                lambda: v[a : a + n, :, c].reshape(n * TOK, HEAD),
                n * TOK, None,
            )],
            TOK, None, finish,
        )

    def local_head(h, _):
        @pl.when(h % PER == 0)
        def _():
            for cp in loads(h // PER):
                cp.wait()

        run([local_unit(h, i) for i in range(4)])
        for at, fn in (
            (2, service_a),
            (3, service_q),
            (5, lambda: service_ring(0, 1)),
            (6, lambda: service_ring(1, 1)),
            (8, lambda: service_ring(0, 2)),
            (9, lambda: service_ring(1, 2)),
        ):
            pl.when(h == at)(fn)
        return 0

    lax.fori_loop(0, HEADS, local_head, 0)

    def pick(kind, dst, place, half):
        for side in range(2):
            kf = nb_s[place, side, 0]
            blk = rings[kind][2 * (kf % 4) + half, kf // 4]
            for ch in range(CHUNKS):
                dst[ch, side] = blk[:, ch * WIDE : (ch + 1) * WIDE]

    def pick_all(kind):
        snd, got = ((sndk, gotk), (sndv, gotv))[kind]
        pick(kind, snd.at[0], 0, 0)
        pick(kind, snd.at[1], 0, 1)
        for i in range(1, 5):
            pick(kind, snd.at[1 + i], i, (i + 1) % 2)

    def pick_own(kind):
        got = (gotk, gotv)[kind]
        pick(kind, got.at[0], 5, 0)
        pick(kind, got.at[1], 5, 1)

    def k_copy(i):
        if i == 0:
            return remote(sndk.at[0:2], gotk.at[2:4], sk_ss.at[0], sk_rs.at[0], sel[0])
        return remote(sndk.at[1 + i], gotk.at[3 + i], sk_ss.at[i], sk_rs.at[i], sel[i])

    def v_copy(ch, i):
        if i == 0:
            return remote(sndv.at[0:2, ch], gotv.at[2:4, ch], sv_ss.at[ch, 0], sv_rs.at[ch, 0], sel[0])
        return remote(sndv.at[1 + i, ch], gotv.at[3 + i, ch], sv_ss.at[ch, i], sv_rs.at[ch, i], sel[i])

    service_ring(0, 3)
    service_ring(1, 3)
    for part in (2, 3):
        for cp in ring_copies(part, 0):
            cp.start()
    for i in range(5):
        remote(nb.at[i], nb.at[i], nb_ss.at[i], nb_rs.at[i], zr).wait_recv()
    nb_smem = pltpu.make_async_copy(nb, nb_s, loc_sem.at[2])
    nb_smem.start()
    nb_smem.wait()
    for part in (0, 1):
        for cp in ring_copies(part, 3):
            cp.wait_recv()
    pick_all(0)
    for i in range(5):
        k_copy(i).start()
    for s in (1, 2, 3):
        service_ring(2, s)
        service_ring(3, s)
        if s == 1:
            pick_own(0)
    for part in (2, 3):
        for cp in ring_copies(part, 3):
            cp.wait_recv()
    pick_all(1)
    for ch in range(CHUNKS):
        for i in range(5):
            v_copy(ch, i).start()
    pick_own(1)

    for cp in edge_copies:
        cp.wait_recv()

    def forward(e):
        for ch in range(CHUNKS):
            for kind in range(2):
                fwd_copy(e, ch, kind).start()

    each_end(forward)

    for n, (a, b) in enumerate(quad):
        g = quad_gid(a, b)
        remote(qx.at[g], qx.at[g], qx_ss.at[n], qx_rs.at[g], zr).wait_recv()
    st_s[...] = jnp.zeros_like(st_s)

    def joint_unit(h):
        c = cs(h)

        def finish(m, l, o):
            l = jnp.sum(l, axis=1, keepdims=True)
            ox_s[:, :, c] = (o / l).astype(BF16).reshape(4, 32, HEAD)
            lane = lax.broadcasted_iota(jnp.int32, (128, HEAD), 1) == h
            st_s[:, 0] = jnp.where(lane, m, st_s[:, 0].reshape(128, HEAD)).reshape(4, 32, HEAD)
            st_s[:, 1] = jnp.where(lane, l, st_s[:, 1].reshape(128, HEAD)).reshape(4, 32, HEAD)

        return unit(
            lambda: qx[:, :, c].reshape(128, HEAD),
            [(
                lambda: ringk[:, :, :, c].reshape(512, HEAD),
                lambda: ringv[:, :, :, c].reshape(512, HEAD),
                512, None,
            )],
            128, None, finish,
        )

    def joint_chunk(ch, _):
        run([joint_unit(ch * PER + j) for j in range(PER)])
        return 0

    lax.fori_loop(0, CHUNKS, joint_chunk, 0)
    ox_copies, st_copies = [], []
    for n, (a, b) in enumerate(quad):
        g = quad_gid(a, b)
        ox_copies.append(remote(ox_s.at[g], ox_r.at[gid], ox_ss.at[n], ox_rs.at[gid], quad_dev(a, b)))
        st_copies.append(remote(st_s.at[g], st_r.at[gid], st_ss.at[n], st_rs.at[gid], quad_dev(a, b)))
    for cp in ox_copies + st_copies:
        cp.start()
    ox_r[gid] = ox_s[gid]
    st_r[gid] = st_s[gid]

    def out_copy(ch):
        c = pl.ds(pl.multiple_of(ch * WIDE, WIDE), WIDE)
        return pltpu.make_async_copy(out_v.at[:, :, c], out_hbm.at[:, :, c], out_sem.at[ch])

    before = jnp.where(x == 0, 2, 0)
    after = jnp.where(x == XN - 1, 3, 1)

    def last_unit(ch, j, i):
        h = ch * PER + j
        c = cs(h)
        w = slice(j * HEAD, (j + 1) * HEAD)

        def finish(m, l, o):
            out_v[i, :, c] = (o * (1.0 / jnp.sum(l, axis=1, keepdims=True))).astype(BF16)

        parts = [(
            lambda: gotk[:, ch, :, :, w].reshape(512, HEAD),
            lambda: gotv[:, ch, :, :, w].reshape(512, HEAD),
            512, None,
        )]
        if i == 0:
            parts.append((lambda: edge[before, 0, :, c], lambda: edge[before, 1, :, c], TOK, f > 0))
        if i == 3:
            parts.append((lambda: edge[after, 0, :, c], lambda: edge[after, 1, :, c], TOK, f < groups - 1))
        state = (lambda: m_st[h, i], lambda: l_st[h, i], lambda: o_st[h, i])
        return unit(lambda: q[i, :, c], parts, TOK, state, finish)

    def last_chunk(ch, _):
        for i in range(5):
            v_copy(ch, i).wait_recv()

        def arrived(e):
            for kind in range(2):
                fwd_copy(e, ch, kind).wait_recv()

        each_end(arrived)
        run([last_unit(ch, j, i) for j in range(PER) for i in range(4)])
        out_copy(ch).start()
        return 0

    for i in range(5):
        k_copy(i).wait_recv()
    lax.fori_loop(0, CHUNKS, last_chunk, 0)

    for n, (a, b) in enumerate(quad):
        g = quad_gid(a, b)
        remote(ox_r.at[g], ox_r.at[g], ox_ss.at[n], ox_rs.at[g], zr).wait_recv()
        remote(st_r.at[g], st_r.at[g], st_ss.at[n], st_rs.at[g], zr).wait_recv()
    m_all = st_r[:, 0]
    w_all = jnp.exp2((m_all - jnp.max(m_all, axis=0, keepdims=True)) * SCALE) * st_r[:, 1]
    total = jnp.sum(w_all, axis=0, keepdims=True)
    w_all = w_all / jnp.where(total > 0, total, 1.0)
    for h in range(HEADS):
        acc = jnp.zeros((32, HEAD), F32)
        for cl in range(4):
            acc = acc + ox_r[cl, :, h * HEAD : (h + 1) * HEAD].astype(F32) * w_all[cl, :, h : h + 1]
        kout[:, h * HEAD : (h + 1) * HEAD] = acc.astype(BF16)

    for cp in a_copies + aq_copies + nb_copies + edge_copies + qx_copies + ox_copies + st_copies:
        cp.wait_send()

    @pl.when(jnp.logical_not(stays))
    def _():
        a_self.wait_send()

    def forwarded(e):
        for ch in range(CHUNKS):
            for kind in range(2):
                fwd_copy(e, ch, kind).wait_send()

    each_end(forwarded)
    for part in range(4):
        for s in range(4):
            for cp in ring_copies(part, s):
                cp.wait_send()
    for i in range(5):
        k_copy(i).wait_send()
    for ch in range(CHUNKS):
        for i in range(5):
            v_copy(ch, i).wait_send()
        out_copy(ch).wait()


def local(frame_q, frame_k, frame_v, keyframe_q, keyframe_k, keyframe_v, neighbours):
    dma = pltpu.SemaphoreType.DMA
    any_ = pl.BlockSpec(memory_space=pl.ANY)
    whole = pl.BlockSpec(memory_space=pltpu.VMEM)
    vm = pltpu.VMEM
    frame_out, keyframe_out = pl.pallas_call(
        kernel,
        out_shape=(
            jax.ShapeDtypeStruct(frame_q.shape, BF16),
            jax.ShapeDtypeStruct((32, FEAT), BF16),
        ),
        in_specs=[any_] * 3 + [whole] * 3 + [pl.BlockSpec(memory_space=pltpu.SMEM)],
        out_specs=(any_, whole),
        scratch_shapes=[
            vm((4, TOK, FEAT), BF16), vm((4, TOK, FEAT), BF16), vm((4, TOK, FEAT), BF16),
            vm((4, 2, TOK, FEAT), BF16),
            vm((16, HN * FEAT), BF16), vm((8, HN * FEAT), F32),
            vm((8, 16, FEAT), BF16), vm((HN, 8, FEAT), F32),
            vm((ZN, YN, 32, FEAT), BF16), vm((ZN, YN, 32, FEAT), BF16),
            vm((6, CHUNKS, 2, 32, WIDE), BF16), vm((6, CHUNKS, 2, 32, WIDE), BF16),
            vm((8, CHUNKS, 2, 32, WIDE), BF16), vm((8, CHUNKS, 2, 32, WIDE), BF16),
            vm((HEADS, 4, TOK, HEAD), F32), vm((HEADS, 4, TOK, HEAD), F32), vm((HEADS, 4, TOK, HEAD), F32),
            vm((2, TOK, 3 * TOK), F32), vm((2, TOK, HEAD), F32),
            vm((4, TOK, FEAT), BF16),
            vm((4, 32, FEAT), BF16), vm((4, 32, FEAT), BF16), vm((4, 32, FEAT), BF16),
            vm((4, 2, 32, HEAD), F32), vm((4, 2, 32, HEAD), F32),
            vm((8, 128), jnp.int32), vm((6, 8, 128), jnp.int32), pltpu.SMEM((6, 8, 128), jnp.int32),
            dma((CHUNKS, 3)), dma((CHUNKS,)), dma((2, 2)), dma((2, 2)), dma((CHUNKS, 2)), dma((CHUNKS, 2)),
            dma((8,)), dma((8,)), dma((4,)), dma((4,)), dma((5,)), dma((5,)), dma((3,)),
            dma((2, 4, 4)), dma((2, 4, 4)), dma((5,)), dma((5,)), dma((CHUNKS, 5)), dma((CHUNKS, 5)),
            dma((3,)), dma((4,)), dma((3,)), dma((4,)), dma((3,)), dma((4,)),
        ],
        compiler_params=pltpu.CompilerParams(
            collective_id=0, has_side_effects=True, vmem_limit_bytes=60 * 2**20
        ),
    )(frame_q, frame_k, frame_v, keyframe_q, keyframe_k, keyframe_v, neighbours)
    return frame_out, keyframe_out


def solution(mesh):
    placed = (
        P("frames", None, "heads"),
        P("frames", None, "heads"),
        P("frames", None, "heads"),
        P(("frames", "heads"), None),
        P(("frames", "heads"), None),
        P(("frames", "heads"), None),
        P("frames", None),
    )
    return jax.shard_map(
        local,
        mesh=mesh,
        in_specs=placed,
        out_specs=(P("frames", None, "heads"), P("frames", "heads")),
        check_vma=False,
    )
```

```python
import math

import jax
import jax.numpy as jnp
from jax import lax
from jax.experimental import pallas as pl
from jax.experimental.pallas import tpu as pltpu
from jax.sharding import PartitionSpec as P

HEAD = 128
XN, ZN, YN = 4, 8, 2
HN = 4
HEADS = 10
CHUNKS = 5
WIDE = 256
PER = WIDE // HEAD
TOK = 256
HALF = TOK // 2
SEGS = ((0, 768, (0, 1, 2)), (768, 512, (3, 4)))
FEAT = HEADS * HEAD
SCALE = math.log2(math.e) / math.sqrt(HEAD)
F32 = jnp.float32
BF16 = jnp.bfloat16
NT = (((1,), (1,)), ((), ()))
SPANS = ((0, 2), (0, 3), (1, 3), (2, 2))
MESH = pl.DeviceIdType.MESH


def kernel(
    q_hbm, k_hbm, v_hbm, kf_q, kf_k, kf_v, ids,
    out_hbm, kout,
    q, k, v, edge, kv, kq, arr, arrq, rka, rkb, rva, rvb, rbuf, sndk, sndv, gotk, gotv,
    o_st, m_st, l_st, sc, sc_m, out_v, qx, ox_s, ox_r, st_s, st_r, nb_v, nb, nb_s,
    load_sem, out_sem, edge_ss, edge_rs, fwd_ss, fwd_rs, up_ss, up_rs, on_ss, on_rs, a_ss, a_rs, aq_ss, aq_rs, nb_ss, nb_rs, loc_sem,
    r_ss, r_rs, sk_ss, sk_rs, sv_ss, sv_rs, qx_ss, qx_rs, ox_ss, ox_rs, st_ss, st_rs,
):
    f = lax.axis_index("frames")
    hd = lax.axis_index("heads")
    x = f % XN
    z = (f // XN) % ZN
    y = f // (XN * ZN)
    xp = x % 2
    groups = XN * ZN * YN

    def dev(y_, z_, x_, h_):
        return ((y_ * ZN + z_) * XN + x_, h_)

    def remote(src, dst, ss, rs, to):
        return pltpu.make_async_remote_copy(
            src_ref=src, dst_ref=dst, send_sem=ss, recv_sem=rs, device_id=to, device_id_type=MESH
        )

    def loads(ch):
        c = pl.ds(pl.multiple_of(ch * WIDE, WIDE), WIDE)
        return [
            pltpu.make_async_copy(a.at[:, :, c], b.at[:, :, c], load_sem.at[ch, n])
            for n, (a, b) in enumerate(((q_hbm, q), (k_hbm, k), (v_hbm, v)))
        ]

    for ch in range(CHUNKS):
        for cp in loads(ch):
            cp.start()

    zr = dev(y, (z + 1) % ZN, x, hd)
    zl = dev(y, (z + ZN - 1) % ZN, x, hd)
    fwd_to = (((f + XN) % groups, hd), ((f + groups - XN) % groups, hd))
    yo = (y + 1) % YN
    right, left = (x + 1) % XN, (x + XN - 1) % XN
    sel = [dev(yo, z, x, hd), dev(y, z, right, hd), dev(y, z, left, hd), dev(yo, z, right, hd), dev(yo, z, left, hd)]
    back = (0, 2, 1, 4, 3)
    barrier = pltpu.get_barrier_semaphore()
    near = []
    me16 = y * HN + hd
    for d in range(1, 16):
        o = (me16 + d) % 8
        near.append(dev(o // HN, z, (x + 2 * (d // 8)) % XN, o % HN))
    partners = near + sel[1:] + [zr, zl] + list(fwd_to)
    for p_ in partners:
        pl.semaphore_signal(barrier, inc=1, device_id=p_, device_id_type=MESH)

    kv[...] = jnp.concatenate([kf_k[...].astype(F32), kf_v[...].astype(F32)], 0).astype(BF16)
    kq[...] = kf_q[...].astype(F32)
    row = lax.broadcasted_iota(jnp.int32, (8, 128), 0)
    nb_v[...] = jnp.where(row == 0, ids[0, 0], ids[0, 1])
    pl.semaphore_wait(barrier, len(partners))

    def cols(h_):
        return pl.ds(pl.multiple_of(h_ * FEAT, FEAT), FEAT)

    ys, hp = hd // 2, hd % 2

    def a_copy(i, xs, h_):
        slot = y * 4 + xs * 2 + hp
        return remote(
            kv.at[:, cols(h_)], arr.at[slot], a_ss.at[i], a_rs.at[slot], dev(ys, z, (x + 2 * xs) % XN, h_)
        )

    a_copies = [a_copy(d, 0, (hd + d) % HN) for d in range(1, HN)] + [a_copy(4 + d, 1, d) for d in range(HN)]
    a_self = a_copy(0, 0, hd)
    own_slot = y * 4 + hp
    a_here = pltpu.make_async_copy(kv.at[:, cols(hd)], arr.at[own_slot], a_rs.at[own_slot])
    stays = ys == y

    for cp in a_copies:
        cp.start()

    @pl.when(stays)
    def _():
        a_here.start()

    @pl.when(jnp.logical_not(stays))
    def _():
        a_self.start()

    aq_copies = [
        remote(kq.at[:, cols((hd + d) % HN)], arrq.at[hd], aq_ss.at[d], aq_rs.at[hd], dev(y, z, x, (hd + d) % HN))
        for d in range(1, HN)
    ]
    nb_copies = [remote(nb_v, nb.at[back[i]], nb_ss.at[i], nb_rs.at[back[i]], sel[i]) for i in range(5)]
    aq_own = pltpu.make_async_copy(kq.at[:, cols(hd)], arrq.at[hd], loc_sem.at[0])
    nb_own = pltpu.make_async_copy(nb_v, nb.at[5], loc_sem.at[1])
    for cp in aq_copies + nb_copies + [aq_own, nb_own]:
        cp.start()

    lo, hi = pl.ds(0, HALF), pl.ds(HALF, HALF)
    kv_hbm = (k_hbm, v_hbm)

    def edge_copy(e, kind, part):
        rows = (lo, hi)[part]
        return remote(
            kv_hbm[kind].at[3 - 3 * e, rows], edge.at[e, kind, rows],
            edge_ss.at[e, kind, part], edge_rs.at[e, kind, part], sel[1 + e],
        )

    first_x, last_x = x == 0, x == XN - 1
    sends_past = (last_x, first_x)
    takes_past = (first_x, last_x)

    def when_not(cond, fn):
        pl.when(jnp.logical_not(cond))(fn)

    for kind in range(2):
        for e in range(2):
            edge_copy(e, kind, 0).start()
            when_not(sends_past[e], lambda: edge_copy(e, kind, 1).start())

    def chunk_cols(ch):
        return pl.ds(pl.multiple_of(ch * WIDE, WIDE), WIDE)

    def fwd_copy(e, ch, kind):
        c = chunk_cols(ch)
        return remote(
            edge.at[e, kind, lo, c], edge.at[2 + e, kind, lo, c], fwd_ss.at[ch, kind], fwd_rs.at[ch, kind], fwd_to[e]
        )

    def up_copy(e, ch, kind):
        c = chunk_cols(ch)
        return remote(
            kv_hbm[kind].at[3 - 3 * e, hi, c], rbuf.at[kind, :, c], up_ss.at[ch, kind], up_rs.at[ch, kind], fwd_to[e]
        )

    def on_copy(e, ch, kind):
        c = chunk_cols(ch)
        return remote(
            rbuf.at[kind, :, c], edge.at[2 + e, kind, hi, c], on_ss.at[ch, kind], on_rs.at[ch, kind], sel[1 + e]
        )

    def each(conds, fn):
        for e in range(2):
            pl.when(conds[e])(lambda: fn(e))

    rings = (rka, rkb, rva, rvb)

    def ring_copies(part, s):
        r = rings[part]
        a = (z + ZN - s) % ZN
        b = (z + s) % ZN
        src_r = r.at[a] if s < 3 else r.at[a, :, 0:16]
        src_l = r.at[b] if s < 3 else r.at[b, :, 16:32]
        return (
            remote(src_r, src_r, r_ss.at[0, part, s], r_rs.at[0, part, s], zr),
            remote(src_l, src_l, r_ss.at[1, part, s], r_rs.at[1, part, s], zl),
        )

    quad = [(a, b) for a, b in ((0, 1), (1, 0), (1, 1))]
    gid = xp * 2 + y

    def quad_dev(a, b):
        return dev((y + b) % 2, z, x - xp + (xp + a) % 2, hd)

    def quad_gid(a, b):
        return ((xp + a) % 2) * 2 + (y + b) % 2

    qx_copies = [
        remote(qx.at[gid], qx.at[gid], qx_ss.at[n], qx_rs.at[gid], quad_dev(a, b)) for n, (a, b) in enumerate(quad)
    ]

    def service_a():
        for slot in range(8):
            remote(arr.at[slot], arr.at[slot], a_ss.at[slot], a_rs.at[slot], zr).wait_recv()
        for ysrc in range(YN):
            for j in range(2):
                t0 = arr[ysrc * 4 + 2 * j].astype(F32)
                t1 = arr[ysrc * 4 + 2 * j + 1].astype(F32)
                r = pl.ds(16 * j, 16)
                both = (jnp.concatenate([t0[:8], t1[:8]], 0), jnp.concatenate([t0[8:], t1[8:]], 0))
                for part in range(4):
                    first, width, _ = SEGS[part % 2]
                    rings[part][z, ysrc, r] = both[part // 2][:, first : first + width].astype(BF16)
        begin(0)
        begin(1)

    def begin(part):
        for cp in ring_copies(part, 0):
            cp.start()

    def service_q():
        aq_own.wait()
        nb_own.wait()
        for d in range(1, HN):
            h4 = (hd + d) % HN
            remote(arrq.at[h4], arrq.at[h4], aq_ss.at[d], aq_rs.at[h4], zr).wait_recv()
        for j in range(HN // 2):
            qx[gid, pl.ds(16 * j, 16)] = jnp.concatenate([arrq[2 * j], arrq[2 * j + 1]], 0).astype(BF16)
        for cp in qx_copies:
            cp.start()

    def service_ring(part, s):
        for cp in ring_copies(part, s - 1):
            cp.wait_recv()
        for cp in ring_copies(part, s):
            cp.start()

    def cs(h):
        return pl.ds(pl.multiple_of(h * HEAD, HEAD), HEAD)

    def run(units):
        units[0][0](0)
        for j in range(len(units)):
            if j + 1 < len(units):
                units[j + 1][0]((j + 1) % 2)
            units[j][1](j % 2)

    def unit(get_q, parts, rows, fold, finish):
        def scores(slot):
            qq = get_q()
            at, top = 0, None
            for get_k, _, n, valid in parts:
                s = lax.dot_general(qq, get_k(), NT, preferred_element_type=F32)
                if valid is not None:
                    s = jnp.where(valid, s, -jnp.inf)
                sc[slot, 0:rows, at : at + n] = s
                for t in range(0, n, HEAD):
                    piece = s[:, t : t + HEAD]
                    top = piece if top is None else jnp.maximum(top, piece)
                at += n
            m = jnp.broadcast_to(jnp.max(top, axis=1, keepdims=True), (rows, HEAD))
            if fold is not None:
                m = jnp.maximum(m, fold[0]())
            sc_m[slot, 0:rows] = m

        def values(slot):
            m = sc_m[slot, 0:rows]
            at, l, o = 0, None, None
            for _, get_v, n, _ in parts:
                ps = []
                for t in range(at, at + n, HEAD):
                    p = jnp.exp2((sc[slot, 0:rows, t : t + HEAD] - m) * SCALE)
                    l = p if l is None else l + p
                    ps.append(p.astype(BF16))
                d = jnp.dot(jnp.concatenate(ps, axis=1), get_v(), preferred_element_type=F32)
                o = d if o is None else o + d
                at += n
            if fold is not None:
                a = jnp.exp2((fold[0]() - m) * SCALE)
                l = l + fold[1]() * a
                o = o + fold[2]() * a
            finish(m, l, o)

        return scores, values

    def local_unit(h, i):
        a, n = SPANS[i]
        c = cs(h)

        def finish(m, l, o):
            m_st[h, i] = m
            l_st[h, i] = l
            o_st[h, i] = o

        return unit(
            lambda: q[i, :, c],
            [(
                lambda: k[a : a + n, :, c].reshape(n * TOK, HEAD),
                lambda: v[a : a + n, :, c].reshape(n * TOK, HEAD),
                n * TOK, None,
            )],
            TOK, None, finish,
        )

    def local_head(h, _):
        @pl.when(h % PER == 0)
        def _():
            for cp in loads(h // PER):
                cp.wait()

        run([local_unit(h, i) for i in range(4)])
        for at, fns in (
            (1, (service_a,)),
            (2, (service_q,)),
            (3, (lambda: service_ring(0, 1),)),
            (4, (lambda: service_ring(1, 1),)),
            (5, (lambda: service_ring(0, 2),)),
            (6, (lambda: service_ring(1, 2), lambda: begin(2))),
            (7, (lambda: service_ring(0, 3),)),
            (8, (lambda: service_ring(1, 3),)),
            (9, (lambda: service_ring(2, 1),)),
        ):
            @pl.when(h == at)
            def _():
                for fn in fns:
                    fn()
        return 0

    lax.fori_loop(0, HEADS, local_head, 0)

    def pick(kind, seg, dst, place, half):
        for side in range(2):
            kf = nb_s[place, side, 0]
            blk = rings[kind * 2 + seg][2 * (kf % 4) + half, kf // 4]
            for n, ch in enumerate(SEGS[seg][2]):
                dst[ch, side] = blk[:, n * WIDE : (n + 1) * WIDE]

    def pick_all(kind, seg):
        snd = (sndk, sndv)[kind]
        pick(kind, seg, snd.at[0], 0, 0)
        pick(kind, seg, snd.at[1], 0, 1)
        for i in range(1, 5):
            pick(kind, seg, snd.at[1 + i], i, (i + 1) % 2)

    def pick_own(kind, seg):
        got = (gotk, gotv)[kind]
        pick(kind, seg, got.at[0], 5, 0)
        pick(kind, seg, got.at[1], 5, 1)

    def k_copy(i):
        if i == 0:
            return remote(sndk.at[0:2], gotk.at[2:4], sk_ss.at[0], sk_rs.at[0], sel[0])
        return remote(sndk.at[1 + i], gotk.at[3 + i], sk_ss.at[i], sk_rs.at[i], sel[i])

    def v_copy(ch, i):
        if i == 0:
            return remote(sndv.at[0:2, ch], gotv.at[2:4, ch], sv_ss.at[ch, 0], sv_rs.at[ch, 0], sel[0])
        return remote(sndv.at[1 + i, ch], gotv.at[3 + i, ch], sv_ss.at[ch, i], sv_rs.at[ch, i], sel[i])

    def ring_done(part):
        for cp in ring_copies(part, 3):
            cp.wait_recv()

    def send_v(seg):
        pick_all(1, seg)
        for ch in SEGS[seg][2]:
            for i in range(5):
                v_copy(ch, i).start()

    begin(3)
    for i in range(5):
        remote(nb.at[i], nb.at[i], nb_ss.at[i], nb_rs.at[i], zr).wait_recv()
    nb_smem = pltpu.make_async_copy(nb, nb_s, loc_sem.at[2])
    nb_smem.start()
    nb_smem.wait()
    ring_done(0)
    ring_done(1)
    pick_all(0, 0)
    pick_all(0, 1)
    for i in range(5):
        k_copy(i).start()
    service_ring(2, 2)
    service_ring(3, 1)
    pick_own(0, 0)
    pick_own(0, 1)
    service_ring(2, 3)
    service_ring(3, 2)
    ring_done(2)
    send_v(0)
    service_ring(3, 3)

    for kind in range(2):
        for e in range(2):
            edge_copy(e, kind, 0).wait_recv()

    def all_chunks(fn):
        for ch in range(CHUNKS):
            for kind in range(2):
                fn(ch, kind)

    each(takes_past, lambda e: all_chunks(lambda ch, kind: fwd_copy(e, ch, kind).start()))
    each(sends_past, lambda e: all_chunks(lambda ch, kind: up_copy(e, ch, kind).start()))
    ring_done(3)
    send_v(1)
    pick_own(1, 0)
    pick_own(1, 1)

    for n, (a, b) in enumerate(quad):
        g = quad_gid(a, b)
        remote(qx.at[g], qx.at[g], qx_ss.at[n], qx_rs.at[g], zr).wait_recv()
    st_s[...] = jnp.zeros_like(st_s)

    def joint_unit(seg, h):
        c = cs(h)
        w = cs(h - SEGS[seg][0] // HEAD)

        def finish(m, l, o):
            l = jnp.sum(l, axis=1, keepdims=True)
            ox_s[:, :, c] = (o / l).astype(BF16).reshape(4, 32, HEAD)
            lane = lax.broadcasted_iota(jnp.int32, (128, HEAD), 1) == h
            st_s[:, 0] = jnp.where(lane, m, st_s[:, 0].reshape(128, HEAD)).reshape(4, 32, HEAD)
            st_s[:, 1] = jnp.where(lane, l, st_s[:, 1].reshape(128, HEAD)).reshape(4, 32, HEAD)

        return unit(
            lambda: qx[:, :, c].reshape(128, HEAD),
            [(
                lambda: rings[seg][:, :, :, w].reshape(512, HEAD),
                lambda: rings[2 + seg][:, :, :, w].reshape(512, HEAD),
                512, None,
            )],
            128, None, finish,
        )

    for seg in range(2):
        first, width, _ = SEGS[seg]

        def joint_step(n, _):
            run([joint_unit(seg, first // HEAD + n * PER + j) for j in range(PER)])
            return 0

        lax.fori_loop(0, width // WIDE, joint_step, 0)
    ox_copies, st_copies = [], []
    for n, (a, b) in enumerate(quad):
        g = quad_gid(a, b)
        ox_copies.append(remote(ox_s.at[g], ox_r.at[gid], ox_ss.at[n], ox_rs.at[gid], quad_dev(a, b)))
        st_copies.append(remote(st_s.at[g], st_r.at[gid], st_ss.at[n], st_rs.at[gid], quad_dev(a, b)))
    for cp in ox_copies + st_copies:
        cp.start()
    ox_r[gid] = ox_s[gid]
    st_r[gid] = st_s[gid]

    def out_copy(ch):
        c = pl.ds(pl.multiple_of(ch * WIDE, WIDE), WIDE)
        return pltpu.make_async_copy(out_v.at[:, :, c], out_hbm.at[:, :, c], out_sem.at[ch])

    before = jnp.where(x == 0, 2, 0)
    after = jnp.where(x == XN - 1, 3, 1)

    def last_unit(ch, j, i):
        h = ch * PER + j
        c = cs(h)
        w = slice(j * HEAD, (j + 1) * HEAD)

        def finish(m, l, o):
            out_v[i, :, c] = (o * (1.0 / jnp.sum(l, axis=1, keepdims=True))).astype(BF16)

        parts = [(
            lambda: gotk[:, ch, :, :, w].reshape(512, HEAD),
            lambda: gotv[:, ch, :, :, w].reshape(512, HEAD),
            512, None,
        )]
        if i == 0:
            parts.append((lambda: edge[before, 0, :, c], lambda: edge[before, 1, :, c], TOK, f > 0))
        if i == 3:
            parts.append((lambda: edge[after, 0, :, c], lambda: edge[after, 1, :, c], TOK, f < groups - 1))
        state = (lambda: m_st[h, i], lambda: l_st[h, i], lambda: o_st[h, i])
        return unit(lambda: q[i, :, c], parts, TOK, state, finish)

    def last_chunk(ch, _):
        for i in range(5):
            v_copy(ch, i).wait_recv()

        def hand_on(e):
            for kind in range(2):
                up_copy(e, ch, kind).wait_recv()
                on_copy(e, ch, kind).start()

        def arrived(e):
            for kind in range(2):
                fwd_copy(e, ch, kind).wait_recv()
                on_copy(e, ch, kind).wait_recv()

        each(sends_past, hand_on)
        each(takes_past, arrived)
        run([last_unit(ch, j, i) for j in range(PER) for i in range(4)])
        out_copy(ch).start()
        return 0

    for i in range(5):
        k_copy(i).wait_recv()
    for kind in range(2):
        for e in range(2):
            when_not(takes_past[e], lambda: edge_copy(e, kind, 1).wait_recv())
    lax.fori_loop(0, CHUNKS, last_chunk, 0)

    for n, (a, b) in enumerate(quad):
        g = quad_gid(a, b)
        remote(ox_r.at[g], ox_r.at[g], ox_ss.at[n], ox_rs.at[g], zr).wait_recv()
        remote(st_r.at[g], st_r.at[g], st_ss.at[n], st_rs.at[g], zr).wait_recv()
    m_all = st_r[:, 0]
    w_all = jnp.exp2((m_all - jnp.max(m_all, axis=0, keepdims=True)) * SCALE) * st_r[:, 1]
    total = jnp.sum(w_all, axis=0, keepdims=True)
    w_all = w_all / jnp.where(total > 0, total, 1.0)
    for h in range(HEADS):
        acc = jnp.zeros((32, HEAD), F32)
        for cl in range(4):
            acc = acc + ox_r[cl, :, h * HEAD : (h + 1) * HEAD].astype(F32) * w_all[cl, :, h : h + 1]
        kout[:, h * HEAD : (h + 1) * HEAD] = acc.astype(BF16)

    for cp in a_copies + aq_copies + nb_copies + qx_copies + ox_copies + st_copies:
        cp.wait_send()

    @pl.when(jnp.logical_not(stays))
    def _():
        a_self.wait_send()

    for kind in range(2):
        for e in range(2):
            edge_copy(e, kind, 0).wait_send()
            when_not(sends_past[e], lambda: edge_copy(e, kind, 1).wait_send())
    each(takes_past, lambda e: all_chunks(lambda ch, kind: fwd_copy(e, ch, kind).wait_send()))
    each(sends_past, lambda e: all_chunks(lambda ch, kind: up_copy(e, ch, kind).wait_send()))
    each(sends_past, lambda e: all_chunks(lambda ch, kind: on_copy(e, ch, kind).wait_send()))
    for part in range(4):
        for s in range(4):
            for cp in ring_copies(part, s):
                cp.wait_send()
    for i in range(5):
        k_copy(i).wait_send()
    for ch in range(CHUNKS):
        for i in range(5):
            v_copy(ch, i).wait_send()
        out_copy(ch).wait()


def local(frame_q, frame_k, frame_v, keyframe_q, keyframe_k, keyframe_v, neighbours):
    dma = pltpu.SemaphoreType.DMA
    any_ = pl.BlockSpec(memory_space=pl.ANY)
    whole = pl.BlockSpec(memory_space=pltpu.VMEM)
    vm = pltpu.VMEM
    frame_out, keyframe_out = pl.pallas_call(
        kernel,
        out_shape=(
            jax.ShapeDtypeStruct(frame_q.shape, BF16),
            jax.ShapeDtypeStruct((32, FEAT), BF16),
        ),
        in_specs=[any_] * 3 + [whole] * 3 + [pl.BlockSpec(memory_space=pltpu.SMEM)],
        out_specs=(any_, whole),
        scratch_shapes=[
            vm((4, TOK, FEAT), BF16), vm((4, TOK, FEAT), BF16), vm((4, TOK, FEAT), BF16),
            vm((4, 2, TOK, FEAT), BF16),
            vm((16, HN * FEAT), BF16), vm((8, HN * FEAT), F32),
            vm((8, 16, FEAT), BF16), vm((HN, 8, FEAT), F32),
            vm((ZN, YN, 32, SEGS[0][1]), BF16), vm((ZN, YN, 32, SEGS[1][1]), BF16),
            vm((ZN, YN, 32, SEGS[0][1]), BF16), vm((ZN, YN, 32, SEGS[1][1]), BF16),
            vm((2, HALF, FEAT), BF16),
            vm((6, CHUNKS, 2, 32, WIDE), BF16), vm((6, CHUNKS, 2, 32, WIDE), BF16),
            vm((8, CHUNKS, 2, 32, WIDE), BF16), vm((8, CHUNKS, 2, 32, WIDE), BF16),
            vm((HEADS, 4, TOK, HEAD), F32), vm((HEADS, 4, TOK, HEAD), F32), vm((HEADS, 4, TOK, HEAD), F32),
            vm((2, TOK, 3 * TOK), F32), vm((2, TOK, HEAD), F32),
            vm((4, TOK, FEAT), BF16),
            vm((4, 32, FEAT), BF16), vm((4, 32, FEAT), BF16), vm((4, 32, FEAT), BF16),
            vm((4, 2, 32, HEAD), F32), vm((4, 2, 32, HEAD), F32),
            vm((8, 128), jnp.int32), vm((6, 8, 128), jnp.int32), pltpu.SMEM((6, 8, 128), jnp.int32),
            dma((CHUNKS, 3)), dma((CHUNKS,)), dma((2, 2, 2)), dma((2, 2, 2)), dma((CHUNKS, 2)), dma((CHUNKS, 2)),
            dma((CHUNKS, 2)), dma((CHUNKS, 2)), dma((CHUNKS, 2)), dma((CHUNKS, 2)),
            dma((8,)), dma((8,)), dma((4,)), dma((4,)), dma((5,)), dma((5,)), dma((3,)),
            dma((2, 4, 4)), dma((2, 4, 4)), dma((5,)), dma((5,)), dma((CHUNKS, 5)), dma((CHUNKS, 5)),
            dma((3,)), dma((4,)), dma((3,)), dma((4,)), dma((3,)), dma((4,)),
        ],
        compiler_params=pltpu.CompilerParams(
            collective_id=0, has_side_effects=True, vmem_limit_bytes=60 * 2**20
        ),
    )(frame_q, frame_k, frame_v, keyframe_q, keyframe_k, keyframe_v, neighbours)
    return frame_out, keyframe_out


def solution(mesh):
    placed = (
        P("frames", None, "heads"),
        P("frames", None, "heads"),
        P("frames", None, "heads"),
        P(("frames", "heads"), None),
        P(("frames", "heads"), None),
        P(("frames", "heads"), None),
        P("frames", None),
    )
    return jax.shard_map(
        local,
        mesh=mesh,
        in_specs=placed,
        out_specs=(P("frames", None, "heads"), P("frames", "heads")),
        check_vma=False,
    )
```

```python
import math

import jax
import jax.numpy as jnp
from jax import lax
from jax.experimental import pallas as pl
from jax.experimental.pallas import tpu as pltpu
from jax.sharding import PartitionSpec as P

HEAD = 128
XN, ZN, YN = 4, 8, 2
HN = 4
HEADS = 10
CHUNKS = 5
WIDE = 256
PER = WIDE // HEAD
TOK = 256
HALF = TOK // 2
SEGS = ((0, 512, (0, 1)), (512, 768, (2, 3, 4)))
FEAT = HEADS * HEAD
SCALE = math.log2(math.e) / math.sqrt(HEAD)
F32 = jnp.float32
BF16 = jnp.bfloat16
NT = (((1,), (1,)), ((), ()))
SPANS = ((0, 2), (0, 3), (1, 3), (2, 2))
MESH = pl.DeviceIdType.MESH


def kernel(
    q_hbm, k_hbm, v_hbm, kf_q, kf_k, kf_v, ids,
    out_hbm, kout,
    q, k, v, edge, kv, kq, arr, arrq, rka, rkb, rva, rvb, rbuf, sndk, sndv, gotk, gotv,
    o_st, m_st, l_st, sc, sc_m, out_v, qx, ox_s, ox_r, st_s, st_r, nb_v, nb, nb_s,
    load_sem, out_sem, edge_ss, edge_rs, fwd_ss, fwd_rs, up_ss, up_rs, on_ss, on_rs, a_ss, a_rs, aq_ss, aq_rs, nb_ss, nb_rs, loc_sem,
    r_ss, r_rs, sk_ss, sk_rs, sv_ss, sv_rs, qx_ss, qx_rs, ox_ss, ox_rs, st_ss, st_rs,
):
    f = lax.axis_index("frames")
    hd = lax.axis_index("heads")
    x = f % XN
    z = (f // XN) % ZN
    y = f // (XN * ZN)
    xp = x % 2
    groups = XN * ZN * YN

    def dev(y_, z_, x_, h_):
        return ((y_ * ZN + z_) * XN + x_, h_)

    def remote(src, dst, ss, rs, to):
        return pltpu.make_async_remote_copy(
            src_ref=src, dst_ref=dst, send_sem=ss, recv_sem=rs, device_id=to, device_id_type=MESH
        )

    def loads(ch):
        c = pl.ds(pl.multiple_of(ch * WIDE, WIDE), WIDE)
        return [
            pltpu.make_async_copy(a.at[:, :, c], b.at[:, :, c], load_sem.at[ch, n])
            for n, (a, b) in enumerate(((q_hbm, q), (k_hbm, k), (v_hbm, v)))
        ]

    for ch in range(CHUNKS):
        for cp in loads(ch):
            cp.start()

    zr = dev(y, (z + 1) % ZN, x, hd)
    zl = dev(y, (z + ZN - 1) % ZN, x, hd)
    fwd_to = (((f + XN) % groups, hd), ((f + groups - XN) % groups, hd))
    yo = (y + 1) % YN
    right, left = (x + 1) % XN, (x + XN - 1) % XN
    sel = [dev(yo, z, x, hd), dev(y, z, right, hd), dev(y, z, left, hd), dev(yo, z, right, hd), dev(yo, z, left, hd)]
    back = (0, 2, 1, 4, 3)
    barrier = pltpu.get_barrier_semaphore()
    near = []
    me16 = y * HN + hd
    for d in range(1, 16):
        o = (me16 + d) % 8
        near.append(dev(o // HN, z, (x + 2 * (d // 8)) % XN, o % HN))
    partners = near + sel[1:] + [zr, zl] + list(fwd_to)
    for p_ in partners:
        pl.semaphore_signal(barrier, inc=1, device_id=p_, device_id_type=MESH)

    kv[...] = jnp.concatenate([kf_k[...].astype(F32), kf_v[...].astype(F32)], 0).astype(BF16)
    kq[...] = kf_q[...].astype(F32)
    row = lax.broadcasted_iota(jnp.int32, (8, 128), 0)
    nb_v[...] = jnp.where(row == 0, ids[0, 0], ids[0, 1])
    pl.semaphore_wait(barrier, len(partners))

    def cols(h_):
        return pl.ds(pl.multiple_of(h_ * FEAT, FEAT), FEAT)

    ys, hp = hd // 2, hd % 2

    def a_copy(i, xs, h_):
        slot = y * 4 + xs * 2 + hp
        return remote(
            kv.at[:, cols(h_)], arr.at[slot], a_ss.at[i], a_rs.at[slot], dev(ys, z, (x + 2 * xs) % XN, h_)
        )

    a_copies = [a_copy(d, 0, (hd + d) % HN) for d in range(1, HN)] + [a_copy(4 + d, 1, d) for d in range(HN)]
    a_self = a_copy(0, 0, hd)
    own_slot = y * 4 + hp
    a_here = pltpu.make_async_copy(kv.at[:, cols(hd)], arr.at[own_slot], a_rs.at[own_slot])
    stays = ys == y

    for cp in a_copies:
        cp.start()

    @pl.when(stays)
    def _():
        a_here.start()

    @pl.when(jnp.logical_not(stays))
    def _():
        a_self.start()

    aq_copies = [
        remote(kq.at[:, cols((hd + d) % HN)], arrq.at[hd], aq_ss.at[d], aq_rs.at[hd], dev(y, z, x, (hd + d) % HN))
        for d in range(1, HN)
    ]
    nb_copies = [remote(nb_v, nb.at[back[i]], nb_ss.at[i], nb_rs.at[back[i]], sel[i]) for i in range(5)]
    aq_own = pltpu.make_async_copy(kq.at[:, cols(hd)], arrq.at[hd], loc_sem.at[0])
    nb_own = pltpu.make_async_copy(nb_v, nb.at[5], loc_sem.at[1])
    for cp in aq_copies + nb_copies + [aq_own, nb_own]:
        cp.start()

    lo, hi = pl.ds(0, HALF), pl.ds(HALF, HALF)
    kv_hbm = (k_hbm, v_hbm)

    def edge_copy(e, kind, part):
        rows = (lo, hi)[part]
        return remote(
            kv_hbm[kind].at[3 - 3 * e, rows], edge.at[e, kind, rows],
            edge_ss.at[e, kind, part], edge_rs.at[e, kind, part], sel[1 + e],
        )

    first_x, last_x = x == 0, x == XN - 1
    inner = groups - XN
    sends_past = (last_x, first_x)
    takes_past = (first_x, last_x)
    ups = (last_x & (f < inner), first_x & (f >= XN))
    ons = (last_x & (f >= XN), first_x & (f < inner))
    fwds = (first_x & (f < inner), last_x & (f >= XN))
    ends = (first_x & (f >= XN), last_x & (f < inner))
    cross = (z == ZN - 1, z == 0)
    early_ups, late_ups = [tuple(u & (c if a else jnp.logical_not(c)) for u, c in zip(ups, cross)) for a in (1, 0)]
    early_fwds, late_fwds = [tuple(u & (c if a else jnp.logical_not(c)) for u, c in zip(fwds, cross)) for a in (1, 0)]

    def when_not(cond, fn):
        pl.when(jnp.logical_not(cond))(fn)

    for kind in range(2):
        for e in range(2):
            edge_copy(e, kind, 0).start()
    for kind in range(2):
        for e in range(2):
            when_not(sends_past[e], lambda: edge_copy(e, kind, 1).start())

    def chunk_cols(ch):
        return pl.ds(pl.multiple_of(ch * WIDE, WIDE), WIDE)

    def fwd_copy(e, ch, kind):
        c = chunk_cols(ch)
        return remote(
            edge.at[e, kind, lo, c], edge.at[2 + e, kind, lo, c], fwd_ss.at[ch, kind], fwd_rs.at[ch, kind], fwd_to[e]
        )

    def up_copy(e, ch, kind):
        c = chunk_cols(ch)
        return remote(
            kv_hbm[kind].at[3 - 3 * e, hi, c], rbuf.at[kind, :, c], up_ss.at[ch, kind], up_rs.at[ch, kind], fwd_to[e]
        )

    def on_copy(e, ch, kind):
        c = chunk_cols(ch)
        return remote(
            rbuf.at[kind, :, c], edge.at[2 + e, kind, hi, c], on_ss.at[ch, kind], on_rs.at[ch, kind], sel[1 + e]
        )

    def each(conds, fn):
        for e in range(2):
            pl.when(conds[e])(lambda: fn(e))

    def both_kinds(fn):
        for kind in range(2):
            fn(kind)

    def all_chunks(fn):
        for ch in range(CHUNKS):
            for kind in range(2):
                fn(ch, kind)

    def past_up(ch, where=ups):
        each(where, lambda e: both_kinds(lambda kind: up_copy(e, ch, kind).start()))

    def past_on(ch):
        def one(e, kind):
            up_copy(e, ch, kind).wait_recv()
            on_copy(e, ch, kind).start()

        each(ons, lambda e: both_kinds(lambda kind: one(e, kind)))

    def past_fwd(ch, where):
        each(where, lambda e: both_kinds(lambda kind: fwd_copy(e, ch, kind).start()))

    def first_halves():
        for kind in range(2):
            for e in range(2):
                edge_copy(e, kind, 0).wait_recv()

    past_up(0)
    past_up(1)
    for e, at in ((0, 0), (1, groups - 1)):
        @pl.when(f == at)
        def _():
            edge[2 + e] = jnp.zeros((2, TOK, FEAT), BF16)


    rings = (rka, rkb, rva, rvb)

    def ring_copies(part, s):
        r = rings[part]
        a = (z + ZN - s) % ZN
        b = (z + s) % ZN
        src_r = r.at[a] if s < 3 else r.at[a, :, 0:16]
        src_l = r.at[b] if s < 3 else r.at[b, :, 16:32]
        return (
            remote(src_r, src_r, r_ss.at[0, part, s], r_rs.at[0, part, s], zr),
            remote(src_l, src_l, r_ss.at[1, part, s], r_rs.at[1, part, s], zl),
        )

    quad = [(a, b) for a, b in ((0, 1), (1, 0), (1, 1))]
    gid = xp * 2 + y

    def quad_dev(a, b):
        return dev((y + b) % 2, z, x - xp + (xp + a) % 2, hd)

    def quad_gid(a, b):
        return ((xp + a) % 2) * 2 + (y + b) % 2

    qx_copies = [
        remote(qx.at[gid], qx.at[gid], qx_ss.at[n], qx_rs.at[gid], quad_dev(a, b)) for n, (a, b) in enumerate(quad)
    ]

    def service_a():
        for slot in range(8):
            remote(arr.at[slot], arr.at[slot], a_ss.at[slot], a_rs.at[slot], zr).wait_recv()
        for ysrc in range(YN):
            for j in range(2):
                t0 = arr[ysrc * 4 + 2 * j].astype(F32)
                t1 = arr[ysrc * 4 + 2 * j + 1].astype(F32)
                r = pl.ds(16 * j, 16)
                both = (jnp.concatenate([t0[:8], t1[:8]], 0), jnp.concatenate([t0[8:], t1[8:]], 0))
                for part in range(4):
                    first, width, _ = SEGS[part % 2]
                    rings[part][z, ysrc, r] = both[part // 2][:, first : first + width].astype(BF16)
        begin(0)
        begin(2)

    def begin(part):
        for cp in ring_copies(part, 0):
            cp.start()

    def service_q():
        aq_own.wait()
        nb_own.wait()
        for d in range(1, HN):
            h4 = (hd + d) % HN
            remote(arrq.at[h4], arrq.at[h4], aq_ss.at[d], aq_rs.at[h4], zr).wait_recv()
        for j in range(HN // 2):
            qx[gid, pl.ds(16 * j, 16)] = jnp.concatenate([arrq[2 * j], arrq[2 * j + 1]], 0).astype(BF16)
        for cp in qx_copies:
            cp.start()
        for i in range(5):
            remote(nb.at[i], nb.at[i], nb_ss.at[i], nb_rs.at[i], zr).wait_recv()
        nb_smem = pltpu.make_async_copy(nb, nb_s, loc_sem.at[2])
        nb_smem.start()
        nb_smem.wait()

    def service_ring(part, s):
        for cp in ring_copies(part, s - 1):
            cp.wait_recv()
        for cp in ring_copies(part, s):
            cp.start()

    def cs(h):
        return pl.ds(pl.multiple_of(h * HEAD, HEAD), HEAD)

    def run(units):
        units[0][0](0)
        for j in range(len(units)):
            if j + 1 < len(units):
                units[j + 1][0]((j + 1) % 2)
            units[j][1](j % 2)

    def unit(get_q, parts, rows, fold, finish):
        def scores(slot):
            qq = get_q()
            at, top = 0, None
            for get_k, _, n, valid in parts:
                s = lax.dot_general(qq, get_k(), NT, preferred_element_type=F32)
                if valid is not None:
                    s = jnp.where(valid, s, -jnp.inf)
                sc[slot, 0:rows, at : at + n] = s
                for t in range(0, n, HEAD):
                    piece = s[:, t : t + HEAD]
                    top = piece if top is None else jnp.maximum(top, piece)
                at += n
            m = jnp.broadcast_to(jnp.max(top, axis=1, keepdims=True), (rows, HEAD))
            if fold is not None:
                m = jnp.maximum(m, fold[0]())
            sc_m[slot, 0:rows] = m

        def values(slot):
            m = sc_m[slot, 0:rows]
            at, l, o = 0, None, None
            for _, get_v, n, _ in parts:
                ps = []
                for t in range(at, at + n, HEAD):
                    p = jnp.exp2((sc[slot, 0:rows, t : t + HEAD] - m) * SCALE)
                    l = p if l is None else l + p
                    ps.append(p.astype(BF16))
                d = jnp.dot(jnp.concatenate(ps, axis=1), get_v(), preferred_element_type=F32)
                o = d if o is None else o + d
                at += n
            if fold is not None:
                a = jnp.exp2((fold[0]() - m) * SCALE)
                l = l + fold[1]() * a
                o = o + fold[2]() * a
            finish(m, l, o)

        return scores, values

    def local_unit(h, i):
        a, n = SPANS[i]
        c = cs(h)

        def finish(m, l, o):
            m_st[h, i] = m
            l_st[h, i] = l
            o_st[h, i] = o

        return unit(
            lambda: q[i, :, c],
            [(
                lambda: k[a : a + n, :, c].reshape(n * TOK, HEAD),
                lambda: v[a : a + n, :, c].reshape(n * TOK, HEAD),
                n * TOK, None,
            )],
            TOK, None, finish,
        )

    def local_head(h, _):
        @pl.when(h % PER == 0)
        def _():
            for cp in loads(h // PER):
                cp.wait()

        run([local_unit(h, i) for i in range(4)])
        for at, fns in (
            (1, (service_a,)),
            (2, (service_q,)),
            (3, (lambda: service_ring(0, 1),)),
            (4, (lambda: service_ring(2, 1),)),
            (5, (lambda: service_ring(0, 2),)),
            (6, (lambda: service_ring(2, 2), lambda: begin(1), lambda: past_up(2, early_ups))),
            (7, (lambda: service_ring(0, 3),)),
            (8, (lambda: service_ring(2, 3), lambda: begin(3), lambda: past_on(0), lambda: past_up(3, early_ups))),
            (9, (lambda: service_ring(1, 1), lambda: past_on(1), lambda: past_up(4, early_ups))),
        ):
            @pl.when(h == at)
            def _():
                for fn in fns:
                    fn()
        return 0

    lax.fori_loop(0, HEADS, local_head, 0)

    def pick(kind, seg, dst, place, half):
        for side in range(2):
            kf = nb_s[place, side, 0]
            blk = rings[kind * 2 + seg][2 * (kf % 4) + half, kf // 4]
            for n, ch in enumerate(SEGS[seg][2]):
                dst[ch, side] = blk[:, n * WIDE : (n + 1) * WIDE]

    def pick_all(kind, seg):
        snd = (sndk, sndv)[kind]
        pick(kind, seg, snd.at[0], 0, 0)
        pick(kind, seg, snd.at[1], 0, 1)
        for i in range(1, 5):
            pick(kind, seg, snd.at[1 + i], i, (i + 1) % 2)

    def pick_own(kind, seg):
        got = (gotk, gotv)[kind]
        pick(kind, seg, got.at[0], 5, 0)
        pick(kind, seg, got.at[1], 5, 1)

    def k_copy(seg, i):
        chs = SEGS[seg][2]
        c = slice(chs[0], chs[-1] + 1)
        if i == 0:
            return remote(sndk.at[0:2, c], gotk.at[2:4, c], sk_ss.at[seg, 0], sk_rs.at[seg, 0], sel[0])
        return remote(sndk.at[1 + i, c], gotk.at[3 + i, c], sk_ss.at[seg, i], sk_rs.at[seg, i], sel[i])

    def v_copy(ch, i):
        if i == 0:
            return remote(sndv.at[0:2, ch], gotv.at[2:4, ch], sv_ss.at[ch, 0], sv_rs.at[ch, 0], sel[0])
        return remote(sndv.at[1 + i, ch], gotv.at[3 + i, ch], sv_ss.at[ch, i], sv_rs.at[ch, i], sel[i])

    def ring_done(part):
        for cp in ring_copies(part, 3):
            cp.wait_recv()

    def send_k(seg):
        ring_done(seg)
        pick_all(0, seg)
        for i in range(5):
            k_copy(seg, i).start()

    def send_v(seg):
        ring_done(2 + seg)
        pick_all(1, seg)
        for ch in SEGS[seg][2]:
            for i in range(5):
                v_copy(ch, i).start()

    send_k(0)
    service_ring(3, 1)
    send_v(0)
    first_halves()
    past_fwd(0, early_fwds)
    service_ring(1, 2)
    past_fwd(1, early_fwds)
    service_ring(3, 2)
    past_fwd(2, early_fwds)
    pick_own(0, 0)
    service_ring(1, 3)
    past_fwd(3, early_fwds)
    service_ring(3, 3)
    past_fwd(4, early_fwds)
    for ch in range(CHUNKS):
        past_fwd(ch, late_fwds)
        if ch >= 2:
            past_up(ch, late_ups)
    pick_own(1, 0)
    send_k(1)
    send_v(1)
    pick_own(0, 1)
    pick_own(1, 1)

    for n, (a, b) in enumerate(quad):
        g = quad_gid(a, b)
        remote(qx.at[g], qx.at[g], qx_ss.at[n], qx_rs.at[g], zr).wait_recv()
    st_s[...] = jnp.zeros_like(st_s)

    def joint_unit(seg, h):
        c = cs(h)
        w = cs(h - SEGS[seg][0] // HEAD)

        def finish(m, l, o):
            l = jnp.sum(l, axis=1, keepdims=True)
            ox_s[:, :, c] = (o / l).astype(BF16).reshape(4, 32, HEAD)
            lane = lax.broadcasted_iota(jnp.int32, (128, HEAD), 1) == h
            st_s[:, 0] = jnp.where(lane, m, st_s[:, 0].reshape(128, HEAD)).reshape(4, 32, HEAD)
            st_s[:, 1] = jnp.where(lane, l, st_s[:, 1].reshape(128, HEAD)).reshape(4, 32, HEAD)

        return unit(
            lambda: qx[:, :, c].reshape(128, HEAD),
            [(
                lambda: rings[seg][:, :, :, w].reshape(512, HEAD),
                lambda: rings[2 + seg][:, :, :, w].reshape(512, HEAD),
                512, None,
            )],
            128, None, finish,
        )

    for seg in range(2):
        first, width, _ = SEGS[seg]

        def joint_step(n, _):
            run([joint_unit(seg, first // HEAD + n * PER + j) for j in range(PER)])
            return 0

        lax.fori_loop(0, width // WIDE, joint_step, 0)
    ox_copies, st_copies = [], []
    for n, (a, b) in enumerate(quad):
        g = quad_gid(a, b)
        ox_copies.append(remote(ox_s.at[g], ox_r.at[gid], ox_ss.at[n], ox_rs.at[gid], quad_dev(a, b)))
        st_copies.append(remote(st_s.at[g], st_r.at[gid], st_ss.at[n], st_rs.at[gid], quad_dev(a, b)))
    for cp in ox_copies + st_copies:
        cp.start()
    ox_r[gid] = ox_s[gid]
    st_r[gid] = st_s[gid]

    def out_copy(ch):
        c = pl.ds(pl.multiple_of(ch * WIDE, WIDE), WIDE)
        return pltpu.make_async_copy(out_v.at[:, :, c], out_hbm.at[:, :, c], out_sem.at[ch])

    before = jnp.where(x == 0, 2, 0)
    after = jnp.where(x == XN - 1, 3, 1)

    def last_unit(ch, j, i):
        h = ch * PER + j
        c = cs(h)
        w = slice(j * HEAD, (j + 1) * HEAD)

        def finish(m, l, o):
            out_v[i, :, c] = (o * (1.0 / jnp.sum(l, axis=1, keepdims=True))).astype(BF16)

        parts = [(
            lambda: gotk[:, ch, :, :, w].reshape(512, HEAD),
            lambda: gotv[:, ch, :, :, w].reshape(512, HEAD),
            512, None,
        )]
        if i == 0:
            parts.append((lambda: edge[before, 0, :, c], lambda: edge[before, 1, :, c], TOK, f > 0))
        if i == 3:
            parts.append((lambda: edge[after, 0, :, c], lambda: edge[after, 1, :, c], TOK, f < groups - 1))
        state = (lambda: m_st[h, i], lambda: l_st[h, i], lambda: o_st[h, i])
        return unit(lambda: q[i, :, c], parts, TOK, state, finish)

    def last_chunk(ch, _):
        for n in range(3):
            pl.when(ch == n)(lambda: past_on(n + 2))
        for i in range(5):
            v_copy(ch, i).wait_recv()
        for seg in range(2):
            @pl.when(ch == SEGS[seg][2][0])
            def _():
                for i in range(5):
                    k_copy(seg, i).wait_recv()

        def arrived(e):
            for kind in range(2):
                fwd_copy(e, ch, kind).wait_recv()
                on_copy(e, ch, kind).wait_recv()

        each(ends, arrived)
        run([last_unit(ch, j, i) for j in range(PER) for i in range(4)])
        out_copy(ch).start()
        return 0

    for kind in range(2):
        for e in range(2):
            when_not(takes_past[e], lambda: edge_copy(e, kind, 1).wait_recv())
    lax.fori_loop(0, CHUNKS, last_chunk, 0)

    for n, (a, b) in enumerate(quad):
        g = quad_gid(a, b)
        remote(ox_r.at[g], ox_r.at[g], ox_ss.at[n], ox_rs.at[g], zr).wait_recv()
        remote(st_r.at[g], st_r.at[g], st_ss.at[n], st_rs.at[g], zr).wait_recv()
    m_all = st_r[:, 0]
    w_all = jnp.exp2((m_all - jnp.max(m_all, axis=0, keepdims=True)) * SCALE) * st_r[:, 1]
    total = jnp.sum(w_all, axis=0, keepdims=True)
    w_all = w_all / jnp.where(total > 0, total, 1.0)
    for h in range(HEADS):
        acc = jnp.zeros((32, HEAD), F32)
        for cl in range(4):
            acc = acc + ox_r[cl, :, h * HEAD : (h + 1) * HEAD].astype(F32) * w_all[cl, :, h : h + 1]
        kout[:, h * HEAD : (h + 1) * HEAD] = acc.astype(BF16)

    for cp in a_copies + aq_copies + nb_copies + qx_copies + ox_copies + st_copies:
        cp.wait_send()

    @pl.when(jnp.logical_not(stays))
    def _():
        a_self.wait_send()

    for kind in range(2):
        for e in range(2):
            edge_copy(e, kind, 0).wait_send()
            when_not(sends_past[e], lambda: edge_copy(e, kind, 1).wait_send())
    each(fwds, lambda e: all_chunks(lambda ch, kind: fwd_copy(e, ch, kind).wait_send()))
    each(ups, lambda e: all_chunks(lambda ch, kind: up_copy(e, ch, kind).wait_send()))
    each(ons, lambda e: all_chunks(lambda ch, kind: on_copy(e, ch, kind).wait_send()))
    for part in range(4):
        for s in range(4):
            for cp in ring_copies(part, s):
                cp.wait_send()
    for seg in range(2):
        for i in range(5):
            k_copy(seg, i).wait_send()
    for ch in range(CHUNKS):
        for i in range(5):
            v_copy(ch, i).wait_send()
        out_copy(ch).wait()


def local(frame_q, frame_k, frame_v, keyframe_q, keyframe_k, keyframe_v, neighbours):
    dma = pltpu.SemaphoreType.DMA
    any_ = pl.BlockSpec(memory_space=pl.ANY)
    whole = pl.BlockSpec(memory_space=pltpu.VMEM)
    vm = pltpu.VMEM
    frame_out, keyframe_out = pl.pallas_call(
        kernel,
        out_shape=(
            jax.ShapeDtypeStruct(frame_q.shape, BF16),
            jax.ShapeDtypeStruct((32, FEAT), BF16),
        ),
        in_specs=[any_] * 3 + [whole] * 3 + [pl.BlockSpec(memory_space=pltpu.SMEM)],
        out_specs=(any_, whole),
        scratch_shapes=[
            vm((4, TOK, FEAT), BF16), vm((4, TOK, FEAT), BF16), vm((4, TOK, FEAT), BF16),
            vm((4, 2, TOK, FEAT), BF16),
            vm((16, HN * FEAT), BF16), vm((8, HN * FEAT), F32),
            vm((8, 16, FEAT), BF16), vm((HN, 8, FEAT), F32),
            vm((ZN, YN, 32, SEGS[0][1]), BF16), vm((ZN, YN, 32, SEGS[1][1]), BF16),
            vm((ZN, YN, 32, SEGS[0][1]), BF16), vm((ZN, YN, 32, SEGS[1][1]), BF16),
            vm((2, HALF, FEAT), BF16),
            vm((6, CHUNKS, 2, 32, WIDE), BF16), vm((6, CHUNKS, 2, 32, WIDE), BF16),
            vm((8, CHUNKS, 2, 32, WIDE), BF16), vm((8, CHUNKS, 2, 32, WIDE), BF16),
            vm((HEADS, 4, TOK, HEAD), F32), vm((HEADS, 4, TOK, HEAD), F32), vm((HEADS, 4, TOK, HEAD), F32),
            vm((2, TOK, 3 * TOK), F32), vm((2, TOK, HEAD), F32),
            vm((4, TOK, FEAT), BF16),
            vm((4, 32, FEAT), BF16), vm((4, 32, FEAT), BF16), vm((4, 32, FEAT), BF16),
            vm((4, 2, 32, HEAD), F32), vm((4, 2, 32, HEAD), F32),
            vm((8, 128), jnp.int32), vm((6, 8, 128), jnp.int32), pltpu.SMEM((6, 8, 128), jnp.int32),
            dma((CHUNKS, 3)), dma((CHUNKS,)), dma((2, 2, 2)), dma((2, 2, 2)), dma((CHUNKS, 2)), dma((CHUNKS, 2)),
            dma((CHUNKS, 2)), dma((CHUNKS, 2)), dma((CHUNKS, 2)), dma((CHUNKS, 2)),
            dma((8,)), dma((8,)), dma((4,)), dma((4,)), dma((5,)), dma((5,)), dma((3,)),
            dma((2, 4, 4)), dma((2, 4, 4)), dma((2, 5)), dma((2, 5)), dma((CHUNKS, 5)), dma((CHUNKS, 5)),
            dma((3,)), dma((4,)), dma((3,)), dma((4,)), dma((3,)), dma((4,)),
        ],
        compiler_params=pltpu.CompilerParams(
            collective_id=0, has_side_effects=True, vmem_limit_bytes=60 * 2**20
        ),
    )(frame_q, frame_k, frame_v, keyframe_q, keyframe_k, keyframe_v, neighbours)
    return frame_out, keyframe_out


def solution(mesh):
    placed = (
        P("frames", None, "heads"),
        P("frames", None, "heads"),
        P("frames", None, "heads"),
        P(("frames", "heads"), None),
        P(("frames", "heads"), None),
        P(("frames", "heads"), None),
        P("frames", None),
    )
    return jax.shard_map(
        local,
        mesh=mesh,
        in_specs=placed,
        out_specs=(P("frames", None, "heads"), P("frames", "heads")),
        check_vma=False,
    )
```

```python
import math

import jax
import jax.numpy as jnp
from jax import lax
from jax.experimental import pallas as pl
from jax.experimental.pallas import tpu as pltpu
from jax.sharding import PartitionSpec as P

HEAD = 128
XN, ZN, YN = 4, 8, 2
HN = 4
HEADS = 10
CHUNKS = 5
WIDE = 256
PER = WIDE // HEAD
TOK = 256
HALF = TOK // 2
SEGS = ((0, 512, (0, 1)), (512, 768, (2, 3, 4)))
FEAT = HEADS * HEAD
SCALE = math.log2(math.e) / math.sqrt(HEAD)
F32 = jnp.float32
BF16 = jnp.bfloat16
NT = (((1,), (1,)), ((), ()))
SPANS = ((0, 2), (0, 3), (1, 3), (2, 2))
MESH = pl.DeviceIdType.MESH


def kernel(
    q_hbm, k_hbm, v_hbm, kf_q, kf_k, kf_v, ids,
    out_hbm, kout,
    q, k, v, edge, kv, kq, arr, arrq, rka, rkb, rva, rvb, rbuf, yup, yfw, sndk, sndv, gotk, gotv,
    o_st, m_st, l_st, sc, sc_m, out_v, qx, ox_s, ox_r, st_s, st_r, nb_v, nb, nb_s,
    load_sem, out_sem, edge_ss, edge_rs, fwd_ss, fwd_rs, up_ss, up_rs, on_ss, on_rs, yu_ss, yu_rs, yf_ss, yf_rs, a_ss, a_rs, aq_ss, aq_rs, nb_ss, nb_rs, loc_sem,
    r_ss, r_rs, sk_ss, sk_rs, sv_ss, sv_rs, qx_ss, qx_rs, ox_ss, ox_rs, st_ss, st_rs,
):
    f = lax.axis_index("frames")
    hd = lax.axis_index("heads")
    x = f % XN
    z = (f // XN) % ZN
    y = f // (XN * ZN)
    xp = x % 2
    groups = XN * ZN * YN

    def dev(y_, z_, x_, h_):
        return ((y_ * ZN + z_) * XN + x_, h_)

    def remote(src, dst, ss, rs, to):
        return pltpu.make_async_remote_copy(
            src_ref=src, dst_ref=dst, send_sem=ss, recv_sem=rs, device_id=to, device_id_type=MESH
        )

    def loads(ch):
        c = pl.ds(pl.multiple_of(ch * WIDE, WIDE), WIDE)
        return [
            pltpu.make_async_copy(a.at[:, :, c], b.at[:, :, c], load_sem.at[ch, n])
            for n, (a, b) in enumerate(((q_hbm, q), (k_hbm, k), (v_hbm, v)))
        ]

    for ch in range(CHUNKS):
        for cp in loads(ch):
            cp.start()

    zr = dev(y, (z + 1) % ZN, x, hd)
    zl = dev(y, (z + ZN - 1) % ZN, x, hd)
    fwd_to = (zr, zl)
    yo = (y + 1) % YN
    right, left = (x + 1) % XN, (x + XN - 1) % XN
    sel = [dev(yo, z, x, hd), dev(y, z, right, hd), dev(y, z, left, hd), dev(yo, z, right, hd), dev(yo, z, left, hd)]
    back = (0, 2, 1, 4, 3)
    barrier = pltpu.get_barrier_semaphore()
    near = []
    me16 = y * HN + hd
    for d in range(1, 16):
        o = (me16 + d) % 8
        near.append(dev(o // HN, z, (x + 2 * (d // 8)) % XN, o % HN))
    partners = near + sel[1:] + [zr, zl]
    for p_ in partners:
        pl.semaphore_signal(barrier, inc=1, device_id=p_, device_id_type=MESH)

    kv[...] = jnp.concatenate([kf_k[...].astype(F32), kf_v[...].astype(F32)], 0).astype(BF16)
    kq[...] = kf_q[...].astype(F32)
    row = lax.broadcasted_iota(jnp.int32, (8, 128), 0)
    nb_v[...] = jnp.where(row == 0, ids[0, 0], ids[0, 1])
    pl.semaphore_wait(barrier, len(partners))

    def cols(h_):
        return pl.ds(pl.multiple_of(h_ * FEAT, FEAT), FEAT)

    ys, hp = hd // 2, hd % 2

    def a_copy(i, xs, h_):
        slot = y * 4 + xs * 2 + hp
        return remote(
            kv.at[:, cols(h_)], arr.at[slot], a_ss.at[i], a_rs.at[slot], dev(ys, z, (x + 2 * xs) % XN, h_)
        )

    a_copies = [a_copy(d, 0, (hd + d) % HN) for d in range(1, HN)] + [a_copy(4 + d, 1, d) for d in range(HN)]
    a_self = a_copy(0, 0, hd)
    own_slot = y * 4 + hp
    a_here = pltpu.make_async_copy(kv.at[:, cols(hd)], arr.at[own_slot], a_rs.at[own_slot])
    stays = ys == y

    for cp in a_copies:
        cp.start()

    @pl.when(stays)
    def _():
        a_here.start()

    @pl.when(jnp.logical_not(stays))
    def _():
        a_self.start()

    aq_copies = [
        remote(kq.at[:, cols((hd + d) % HN)], arrq.at[hd], aq_ss.at[d], aq_rs.at[hd], dev(y, z, x, (hd + d) % HN))
        for d in range(1, HN)
    ]
    nb_copies = [remote(nb_v, nb.at[back[i]], nb_ss.at[i], nb_rs.at[back[i]], sel[i]) for i in range(5)]
    aq_own = pltpu.make_async_copy(kq.at[:, cols(hd)], arrq.at[hd], loc_sem.at[0])
    nb_own = pltpu.make_async_copy(nb_v, nb.at[5], loc_sem.at[1])
    for cp in aq_copies + nb_copies + [aq_own, nb_own]:
        cp.start()

    lo, hi = pl.ds(0, HALF), pl.ds(HALF, HALF)
    kv_hbm = (k_hbm, v_hbm)

    def edge_copy(e, kind, part):
        rows = (lo, hi)[part]
        return remote(
            kv_hbm[kind].at[3 - 3 * e, rows], edge.at[e, kind, rows],
            edge_ss.at[e, kind, part], edge_rs.at[e, kind, part], sel[1 + e],
        )

    first_x, last_x = x == 0, x == XN - 1
    inner = groups - XN
    sends_past = (last_x, first_x)
    takes_past = (first_x, last_x)
    ons = (last_x & (f >= XN), first_x & (f < inner))
    ends = (first_x & (f >= XN), last_x & (f < inner))
    wrap = (z == ZN - 1, z == 0)
    near_y, far_y = (y == 0, y == YN - 1), (y == YN - 1, y == 0)
    plain_ups = tuple(u & jnp.logical_not(w) for u, w in zip(sends_past, wrap))
    cross_ups = tuple(u & w & t for u, w, t in zip(sends_past, wrap, near_y))
    stand_ups = tuple(u & w & t for u, w, t in zip(sends_past, wrap, far_y))
    plain_fwds = tuple(u & jnp.logical_not(w) for u, w in zip(takes_past, wrap))
    cross_fwds = tuple(u & w & t for u, w, t in zip(takes_past, wrap, near_y))
    stand_fwds = tuple(u & w & t for u, w, t in zip(takes_past, wrap, far_y))

    def when_not(cond, fn):
        pl.when(jnp.logical_not(cond))(fn)

    for kind in range(2):
        for e in range(2):
            edge_copy(e, kind, 0).start()

    def second_halves(kind):
        for e in range(2):
            when_not(sends_past[e], lambda: edge_copy(e, kind, 1).start())

    def chunk_cols(ch):
        return pl.ds(pl.multiple_of(ch * WIDE, WIDE), WIDE)

    def fwd_copy(e, ch, kind, stand=False):
        c = chunk_cols(ch)
        src = yfw.at[kind, :, c] if stand else edge.at[e, kind, lo, c]
        return remote(
            src, edge.at[2 + e, kind, lo, c], fwd_ss.at[ch, kind], fwd_rs.at[ch, kind], fwd_to[e]
        )

    def up_copy(e, ch, kind, stand=False):
        c = chunk_cols(ch)
        src = yup.at[kind, :, c] if stand else kv_hbm[kind].at[3 - 3 * e, hi, c]
        return remote(
            src, rbuf.at[kind, :, c], up_ss.at[ch, kind], up_rs.at[ch, kind], fwd_to[e]
        )

    def on_copy(e, ch, kind):
        c = chunk_cols(ch)
        return remote(
            rbuf.at[kind, :, c], edge.at[2 + e, kind, hi, c], on_ss.at[ch, kind], on_rs.at[ch, kind], sel[1 + e]
        )

    def each(conds, fn):
        for e in range(2):
            pl.when(conds[e])(lambda: fn(e))

    def both_kinds(fn):
        for kind in range(2):
            fn(kind)

    def all_chunks(fn):
        for ch in range(CHUNKS):
            for kind in range(2):
                fn(ch, kind)

    def yup_copy(e, kind):
        return remote(kv_hbm[kind].at[3 - 3 * e, hi], yup.at[kind], yu_ss.at[kind], yu_rs.at[kind], sel[0])

    def yfw_copy(e, kind):
        return remote(edge.at[e, kind, lo], yfw.at[kind], yf_ss.at[kind], yf_rs.at[kind], sel[0])

    def past_up(ch, stand=False):
        where = stand_ups if stand else plain_ups
        each(where, lambda e: both_kinds(lambda kind: up_copy(e, ch, kind, stand).start()))

    def stand_up_first():
        each(stand_ups, lambda e: both_kinds(lambda kind: yup_copy(e, kind).wait_recv()))
        past_up(0, True)
        past_up(1, True)

    def past_on(ch):
        def one(e, kind):
            up_copy(e, ch, kind).wait_recv()
            on_copy(e, ch, kind).start()

        each(ons, lambda e: both_kinds(lambda kind: one(e, kind)))

    def past_fwd(ch, stand=False):
        where = stand_fwds if stand else plain_fwds
        each(where, lambda e: both_kinds(lambda kind: fwd_copy(e, ch, kind, stand).start()))

    def cross_fwd_start():
        each(cross_fwds, lambda e: both_kinds(lambda kind: yfw_copy(e, kind).start()))

    def first_halves():
        for kind in range(2):
            for e in range(2):
                edge_copy(e, kind, 0).wait_recv()

    each(cross_ups, lambda e: both_kinds(lambda kind: yup_copy(e, kind).start()))
    past_up(0)
    past_up(1)
    for e, at in ((0, 0), (1, groups - 1)):
        @pl.when(f == at)
        def _():
            edge[2 + e] = jnp.zeros((2, TOK, FEAT), BF16)


    rings = (rka, rkb, rva, rvb)

    def ring_copies(part, s):
        r = rings[part]
        a = (z + ZN - s) % ZN
        b = (z + s) % ZN
        src_r = r.at[a] if s < 3 else r.at[a, :, 0:16]
        src_l = r.at[b] if s < 3 else r.at[b, :, 16:32]
        return (
            remote(src_r, src_r, r_ss.at[0, part, s], r_rs.at[0, part, s], zr),
            remote(src_l, src_l, r_ss.at[1, part, s], r_rs.at[1, part, s], zl),
        )

    quad = [(a, b) for a, b in ((0, 1), (1, 0), (1, 1))]
    gid = xp * 2 + y

    def quad_dev(a, b):
        return dev((y + b) % 2, z, x - xp + (xp + a) % 2, hd)

    def quad_gid(a, b):
        return ((xp + a) % 2) * 2 + (y + b) % 2

    qx_copies = [
        remote(qx.at[gid], qx.at[gid], qx_ss.at[n], qx_rs.at[gid], quad_dev(a, b)) for n, (a, b) in enumerate(quad)
    ]

    def service_a():
        for slot in range(8):
            remote(arr.at[slot], arr.at[slot], a_ss.at[slot], a_rs.at[slot], zr).wait_recv()
        for ysrc in range(YN):
            for j in range(2):
                t0 = arr[ysrc * 4 + 2 * j].astype(F32)
                t1 = arr[ysrc * 4 + 2 * j + 1].astype(F32)
                r = pl.ds(16 * j, 16)
                both = (jnp.concatenate([t0[:8], t1[:8]], 0), jnp.concatenate([t0[8:], t1[8:]], 0))
                for part in range(4):
                    first, width, _ = SEGS[part % 2]
                    rings[part][z, ysrc, r] = both[part // 2][:, first : first + width].astype(BF16)
        begin(0)
        begin(2)

    def begin(part):
        for cp in ring_copies(part, 0):
            cp.start()

    def service_q():
        aq_own.wait()
        nb_own.wait()
        for d in range(1, HN):
            h4 = (hd + d) % HN
            remote(arrq.at[h4], arrq.at[h4], aq_ss.at[d], aq_rs.at[h4], zr).wait_recv()
        for j in range(HN // 2):
            qx[gid, pl.ds(16 * j, 16)] = jnp.concatenate([arrq[2 * j], arrq[2 * j + 1]], 0).astype(BF16)
        for cp in qx_copies:
            cp.start()
        for i in range(5):
            remote(nb.at[i], nb.at[i], nb_ss.at[i], nb_rs.at[i], zr).wait_recv()
        nb_smem = pltpu.make_async_copy(nb, nb_s, loc_sem.at[2])
        nb_smem.start()
        nb_smem.wait()

    def service_ring(part, s):
        for cp in ring_copies(part, s - 1):
            cp.wait_recv()
        for cp in ring_copies(part, s):
            cp.start()

    def cs(h):
        return pl.ds(pl.multiple_of(h * HEAD, HEAD), HEAD)

    def run(units):
        units[0][0](0)
        for j in range(len(units)):
            if j + 1 < len(units):
                units[j + 1][0]((j + 1) % 2)
            units[j][1](j % 2)

    def unit(get_q, parts, rows, fold, finish):
        def scores(slot):
            qq = get_q()
            at, top = 0, None
            for get_k, _, n, valid in parts:
                s = lax.dot_general(qq, get_k(), NT, preferred_element_type=F32)
                if valid is not None:
                    s = jnp.where(valid, s, -jnp.inf)
                sc[slot, 0:rows, at : at + n] = s
                for t in range(0, n, HEAD):
                    piece = s[:, t : t + HEAD]
                    top = piece if top is None else jnp.maximum(top, piece)
                at += n
            m = jnp.broadcast_to(jnp.max(top, axis=1, keepdims=True), (rows, HEAD))
            if fold is not None:
                m = jnp.maximum(m, fold[0]())
            sc_m[slot, 0:rows] = m

        def values(slot):
            m = sc_m[slot, 0:rows]
            at, l, o = 0, None, None
            for _, get_v, n, _ in parts:
                ps = []
                for t in range(at, at + n, HEAD):
                    p = jnp.exp2((sc[slot, 0:rows, t : t + HEAD] - m) * SCALE)
                    l = p if l is None else l + p
                    ps.append(p.astype(BF16))
                d = jnp.dot(jnp.concatenate(ps, axis=1), get_v(), preferred_element_type=F32)
                o = d if o is None else o + d
                at += n
            if fold is not None:
                a = jnp.exp2((fold[0]() - m) * SCALE)
                l = l + fold[1]() * a
                o = o + fold[2]() * a
            finish(m, l, o)

        return scores, values

    def local_unit(h, i):
        a, n = SPANS[i]
        c = cs(h)

        def finish(m, l, o):
            m_st[h, i] = m
            l_st[h, i] = l
            o_st[h, i] = o

        return unit(
            lambda: q[i, :, c],
            [(
                lambda: k[a : a + n, :, c].reshape(n * TOK, HEAD),
                lambda: v[a : a + n, :, c].reshape(n * TOK, HEAD),
                n * TOK, None,
            )],
            TOK, None, finish,
        )

    def local_head(h, _):
        @pl.when(h % PER == 0)
        def _():
            for cp in loads(h // PER):
                cp.wait()

        run([local_unit(h, i) for i in range(4)])
        for at, fns in (
            (1, (service_a,)),
            (3, (lambda: service_ring(0, 1),)),
            (4, (lambda: service_ring(2, 1), lambda: second_halves(0))),
            (5, (lambda: service_ring(0, 2), first_halves, cross_fwd_start, service_q)),
            (6, (lambda: service_ring(2, 2), lambda: begin(1), lambda: second_halves(1), stand_up_first)),
            (7, (lambda: service_ring(0, 3),)),
            (8, (lambda: service_ring(2, 3), lambda: begin(3), lambda: past_on(0))),
            (9, (lambda: service_ring(1, 1), lambda: past_on(1))),
        ):
            @pl.when(h == at)
            def _():
                for fn in fns:
                    fn()
        return 0

    lax.fori_loop(0, HEADS, local_head, 0)

    def pick(kind, seg, dst, place, half):
        for side in range(2):
            kf = nb_s[place, side, 0]
            blk = rings[kind * 2 + seg][2 * (kf % 4) + half, kf // 4]
            for n, ch in enumerate(SEGS[seg][2]):
                dst[ch, side] = blk[:, n * WIDE : (n + 1) * WIDE]

    def pick_all(kind, seg):
        snd = (sndk, sndv)[kind]
        pick(kind, seg, snd.at[0], 0, 0)
        pick(kind, seg, snd.at[1], 0, 1)
        for i in range(1, 5):
            pick(kind, seg, snd.at[1 + i], i, (i + 1) % 2)

    def pick_own(kind, seg):
        got = (gotk, gotv)[kind]
        pick(kind, seg, got.at[0], 5, 0)
        pick(kind, seg, got.at[1], 5, 1)

    def k_copy(seg, i):
        chs = SEGS[seg][2]
        c = slice(chs[0], chs[-1] + 1)
        if i == 0:
            return remote(sndk.at[0:2, c], gotk.at[2:4, c], sk_ss.at[seg, 0], sk_rs.at[seg, 0], sel[0])
        return remote(sndk.at[1 + i, c], gotk.at[3 + i, c], sk_ss.at[seg, i], sk_rs.at[seg, i], sel[i])

    def v_copy(ch, i):
        if i == 0:
            return remote(sndv.at[0:2, ch], gotv.at[2:4, ch], sv_ss.at[ch, 0], sv_rs.at[ch, 0], sel[0])
        return remote(sndv.at[1 + i, ch], gotv.at[3 + i, ch], sv_ss.at[ch, i], sv_rs.at[ch, i], sel[i])

    def ring_done(part):
        for cp in ring_copies(part, 3):
            cp.wait_recv()

    def send_k(seg):
        ring_done(seg)
        pick_all(0, seg)
        for i in range(5):
            k_copy(seg, i).start()

    def send_v(seg):
        ring_done(2 + seg)
        pick_all(1, seg)
        for ch in SEGS[seg][2]:
            for i in range(5):
                v_copy(ch, i).start()

    send_k(0)
    service_ring(3, 1)
    send_v(0)
    service_ring(1, 2)
    service_ring(3, 2)
    pick_own(0, 0)
    service_ring(1, 3)
    service_ring(3, 3)
    for ch in range(CHUNKS):
        past_fwd(ch)
        if ch >= 2:
            past_up(ch)
            past_up(ch, True)
    pick_own(1, 0)
    send_k(1)
    send_v(1)
    each(stand_fwds, lambda e: both_kinds(lambda kind: yfw_copy(e, kind).wait_recv()))
    for ch in range(CHUNKS):
        past_fwd(ch, True)
    pick_own(0, 1)
    pick_own(1, 1)

    for n, (a, b) in enumerate(quad):
        g = quad_gid(a, b)
        remote(qx.at[g], qx.at[g], qx_ss.at[n], qx_rs.at[g], zr).wait_recv()
    st_s[...] = jnp.zeros_like(st_s)

    def joint_unit(seg, h):
        c = cs(h)
        w = cs(h - SEGS[seg][0] // HEAD)

        def finish(m, l, o):
            l = jnp.sum(l, axis=1, keepdims=True)
            ox_s[:, :, c] = (o / l).astype(BF16).reshape(4, 32, HEAD)
            lane = lax.broadcasted_iota(jnp.int32, (128, HEAD), 1) == h
            st_s[:, 0] = jnp.where(lane, m, st_s[:, 0].reshape(128, HEAD)).reshape(4, 32, HEAD)
            st_s[:, 1] = jnp.where(lane, l, st_s[:, 1].reshape(128, HEAD)).reshape(4, 32, HEAD)

        return unit(
            lambda: qx[:, :, c].reshape(128, HEAD),
            [(
                lambda: rings[seg][:, :, :, w].reshape(512, HEAD),
                lambda: rings[2 + seg][:, :, :, w].reshape(512, HEAD),
                512, None,
            )],
            128, None, finish,
        )

    for seg in range(2):
        first, width, _ = SEGS[seg]

        def joint_step(n, _):
            run([joint_unit(seg, first // HEAD + n * PER + j) for j in range(PER)])
            return 0

        lax.fori_loop(0, width // WIDE, joint_step, 0)
    ox_copies, st_copies = [], []
    for n, (a, b) in enumerate(quad):
        g = quad_gid(a, b)
        ox_copies.append(remote(ox_s.at[g], ox_r.at[gid], ox_ss.at[n], ox_rs.at[gid], quad_dev(a, b)))
        st_copies.append(remote(st_s.at[g], st_r.at[gid], st_ss.at[n], st_rs.at[gid], quad_dev(a, b)))
    for cp in ox_copies + st_copies:
        cp.start()
    ox_r[gid] = ox_s[gid]
    st_r[gid] = st_s[gid]

    def out_copy(ch):
        c = pl.ds(pl.multiple_of(ch * WIDE, WIDE), WIDE)
        return pltpu.make_async_copy(out_v.at[:, :, c], out_hbm.at[:, :, c], out_sem.at[ch])

    before = jnp.where(x == 0, 2, 0)
    after = jnp.where(x == XN - 1, 3, 1)

    def last_unit(ch, j, i):
        h = ch * PER + j
        c = cs(h)
        w = slice(j * HEAD, (j + 1) * HEAD)

        def finish(m, l, o):
            out_v[i, :, c] = (o * (1.0 / jnp.sum(l, axis=1, keepdims=True))).astype(BF16)

        parts = [(
            lambda: gotk[:, ch, :, :, w].reshape(512, HEAD),
            lambda: gotv[:, ch, :, :, w].reshape(512, HEAD),
            512, None,
        )]
        if i == 0:
            parts.append((lambda: edge[before, 0, :, c], lambda: edge[before, 1, :, c], TOK, f > 0))
        if i == 3:
            parts.append((lambda: edge[after, 0, :, c], lambda: edge[after, 1, :, c], TOK, f < groups - 1))
        state = (lambda: m_st[h, i], lambda: l_st[h, i], lambda: o_st[h, i])
        return unit(lambda: q[i, :, c], parts, TOK, state, finish)

    def last_chunk(ch, _):
        for n in range(3):
            pl.when(ch == n)(lambda: past_on(n + 2))
        for i in range(5):
            v_copy(ch, i).wait_recv()
        for seg in range(2):
            @pl.when(ch == SEGS[seg][2][0])
            def _():
                for i in range(5):
                    k_copy(seg, i).wait_recv()

        def arrived(e):
            for kind in range(2):
                fwd_copy(e, ch, kind).wait_recv()
                on_copy(e, ch, kind).wait_recv()

        each(ends, arrived)
        run([last_unit(ch, j, i) for j in range(PER) for i in range(4)])
        out_copy(ch).start()
        return 0

    for kind in range(2):
        for e in range(2):
            when_not(takes_past[e], lambda: edge_copy(e, kind, 1).wait_recv())
    lax.fori_loop(0, CHUNKS, last_chunk, 0)

    for n, (a, b) in enumerate(quad):
        g = quad_gid(a, b)
        remote(ox_r.at[g], ox_r.at[g], ox_ss.at[n], ox_rs.at[g], zr).wait_recv()
        remote(st_r.at[g], st_r.at[g], st_ss.at[n], st_rs.at[g], zr).wait_recv()
    m_all = st_r[:, 0]
    w_all = jnp.exp2((m_all - jnp.max(m_all, axis=0, keepdims=True)) * SCALE) * st_r[:, 1]
    total = jnp.sum(w_all, axis=0, keepdims=True)
    w_all = w_all / jnp.where(total > 0, total, 1.0)
    for h in range(HEADS):
        acc = jnp.zeros((32, HEAD), F32)
        for cl in range(4):
            acc = acc + ox_r[cl, :, h * HEAD : (h + 1) * HEAD].astype(F32) * w_all[cl, :, h : h + 1]
        kout[:, h * HEAD : (h + 1) * HEAD] = acc.astype(BF16)

    for cp in a_copies + aq_copies + nb_copies + qx_copies + ox_copies + st_copies:
        cp.wait_send()

    @pl.when(jnp.logical_not(stays))
    def _():
        a_self.wait_send()

    for kind in range(2):
        for e in range(2):
            edge_copy(e, kind, 0).wait_send()
            when_not(sends_past[e], lambda: edge_copy(e, kind, 1).wait_send())
    for group in (plain_fwds, stand_fwds):
        each(group, lambda e: all_chunks(lambda ch, kind: fwd_copy(e, ch, kind).wait_send()))
    for group in (plain_ups, stand_ups):
        each(group, lambda e: all_chunks(lambda ch, kind: up_copy(e, ch, kind).wait_send()))
    each(cross_ups, lambda e: both_kinds(lambda kind: yup_copy(e, kind).wait_send()))
    each(cross_fwds, lambda e: both_kinds(lambda kind: yfw_copy(e, kind).wait_send()))
    each(ons, lambda e: all_chunks(lambda ch, kind: on_copy(e, ch, kind).wait_send()))
    for part in range(4):
        for s in range(4):
            for cp in ring_copies(part, s):
                cp.wait_send()
    for seg in range(2):
        for i in range(5):
            k_copy(seg, i).wait_send()
    for ch in range(CHUNKS):
        for i in range(5):
            v_copy(ch, i).wait_send()
        out_copy(ch).wait()


def local(frame_q, frame_k, frame_v, keyframe_q, keyframe_k, keyframe_v, neighbours):
    dma = pltpu.SemaphoreType.DMA
    any_ = pl.BlockSpec(memory_space=pl.ANY)
    whole = pl.BlockSpec(memory_space=pltpu.VMEM)
    vm = pltpu.VMEM
    frame_out, keyframe_out = pl.pallas_call(
        kernel,
        out_shape=(
            jax.ShapeDtypeStruct(frame_q.shape, BF16),
            jax.ShapeDtypeStruct((32, FEAT), BF16),
        ),
        in_specs=[any_] * 3 + [whole] * 3 + [pl.BlockSpec(memory_space=pltpu.SMEM)],
        out_specs=(any_, whole),
        scratch_shapes=[
            vm((4, TOK, FEAT), BF16), vm((4, TOK, FEAT), BF16), vm((4, TOK, FEAT), BF16),
            vm((4, 2, TOK, FEAT), BF16),
            vm((16, HN * FEAT), BF16), vm((8, HN * FEAT), F32),
            vm((8, 16, FEAT), BF16), vm((HN, 8, FEAT), F32),
            vm((ZN, YN, 32, SEGS[0][1]), BF16), vm((ZN, YN, 32, SEGS[1][1]), BF16),
            vm((ZN, YN, 32, SEGS[0][1]), BF16), vm((ZN, YN, 32, SEGS[1][1]), BF16),
            vm((2, HALF, FEAT), BF16), vm((2, HALF, FEAT), BF16), vm((2, HALF, FEAT), BF16),
            vm((6, CHUNKS, 2, 32, WIDE), BF16), vm((6, CHUNKS, 2, 32, WIDE), BF16),
            vm((8, CHUNKS, 2, 32, WIDE), BF16), vm((8, CHUNKS, 2, 32, WIDE), BF16),
            vm((HEADS, 4, TOK, HEAD), F32), vm((HEADS, 4, TOK, HEAD), F32), vm((HEADS, 4, TOK, HEAD), F32),
            vm((2, TOK, 3 * TOK), F32), vm((2, TOK, HEAD), F32),
            vm((4, TOK, FEAT), BF16),
            vm((4, 32, FEAT), BF16), vm((4, 32, FEAT), BF16), vm((4, 32, FEAT), BF16),
            vm((4, 2, 32, HEAD), F32), vm((4, 2, 32, HEAD), F32),
            vm((8, 128), jnp.int32), vm((6, 8, 128), jnp.int32), pltpu.SMEM((6, 8, 128), jnp.int32),
            dma((CHUNKS, 3)), dma((CHUNKS,)), dma((2, 2, 2)), dma((2, 2, 2)), dma((CHUNKS, 2)), dma((CHUNKS, 2)),
            dma((CHUNKS, 2)), dma((CHUNKS, 2)), dma((CHUNKS, 2)), dma((CHUNKS, 2)),
            dma((2,)), dma((2,)), dma((2,)), dma((2,)),
            dma((8,)), dma((8,)), dma((4,)), dma((4,)), dma((5,)), dma((5,)), dma((3,)),
            dma((2, 4, 4)), dma((2, 4, 4)), dma((2, 5)), dma((2, 5)), dma((CHUNKS, 5)), dma((CHUNKS, 5)),
            dma((3,)), dma((4,)), dma((3,)), dma((4,)), dma((3,)), dma((4,)),
        ],
        compiler_params=pltpu.CompilerParams(
            collective_id=0, has_side_effects=True, vmem_limit_bytes=60 * 2**20
        ),
    )(frame_q, frame_k, frame_v, keyframe_q, keyframe_k, keyframe_v, neighbours)
    return frame_out, keyframe_out


def solution(mesh):
    placed = (
        P("frames", None, "heads"),
        P("frames", None, "heads"),
        P("frames", None, "heads"),
        P(("frames", "heads"), None),
        P(("frames", "heads"), None),
        P(("frames", "heads"), None),
        P("frames", None),
    )
    return jax.shard_map(
        local,
        mesh=mesh,
        in_specs=placed,
        out_specs=(P("frames", None, "heads"), P("frames", "heads")),
        check_vma=False,
    )
```
